256 devices in a mesh: px: 16 (over y, x), py: 16 (over z, core).
Axes of the slice: x: 4, y: 4, z: 8, core: 2. Of those that a mesh axis runs over, the one named last changes fastest.
Arguments:
- field: bfloat16 [2, 16, 256, 256, 256], P(None, None, 'px', 'py'), may hold values from -6 to 6
- spectral_weight: float32 [16, 16, 2, 16, 16, 16], P('px', 'py'), may hold values from -1 to 1
- skip_weight: bfloat16 [16, 16], replicated, may hold values from -1.5 to 1.5
- bias: float32 [16], replicated, may hold values from -3 to 3
Outputs:
- output: bfloat16 [2, 16, 256, 256, 256], P(None, None, 'px', 'py')
The draws below stay inside these ranges and needn't reach their ends.
All inputs are finite; a program needn't handle non-finite values.
Results may differ from the reference program's by a relative error of at most 0.014.
Values may be sent and summed in bfloat16 or wider, within the bound.
No kernel may reach another device: no remote copies, remote signals or barrier semaphores. Data moves between devices by JAX's collectives and lax.ppermute only.
A program may use at most 128 MiB of HBM per device.

```python
import math
from functools import partial
import jax
import jax.numpy as jnp
from jax import lax

GRID_X = 256
GRID_Y = 256
GRID_Z = 256
CHANNELS = 16
MODES_X = 16
MODES_Y = 16
MODES_Z = 16
SLICES = 2


def shard_levels(stream_key, extent, split, least, high):
    level = 1.0
    for position, parts in split:
        heights = jax.random.uniform(jax.random.fold_in(jax.random.fold_in(stream_key, 6), position), (parts,), jnp.float32, least / len(split), high / len(split))
        level = level * jnp.repeat(jnp.exp(heights), extent[position] // parts).reshape((-1,) + (1,) * (len(extent) - 1 - position))
    return level


def normal_values(key, shape, scale, most, pieces=(), kind=jnp.bfloat16):
    array = scale * jax.random.normal(key, shape, jnp.float32)
    if pieces:
        array = array * shard_levels(key, shape, pieces, -0.22, 0.18)
    return jnp.clip(array, -most, most).astype(kind)


def setup_inputs(seed: int = 0) -> dict:
    arg_keys = jax.random.split(jax.random.key(seed), 5)
    return {
        "field": normal_values(arg_keys[0], (SLICES, CHANNELS, GRID_X, GRID_Y, GRID_Z), 1.0, 6.0, ((2, 16), (3, 16))),
        "spectral_weight": normal_values(arg_keys[1], (MODES_X, MODES_Y, 2, CHANNELS, CHANNELS, MODES_Z), (2 * CHANNELS) ** -0.5, 1.0, ((0, 16), (1, 16)), jnp.float32),
        "skip_weight": normal_values(arg_keys[2], (CHANNELS, CHANNELS), CHANNELS ** -0.5, 1.5),
        "bias": normal_values(arg_keys[3], (CHANNELS,), 0.5, 3.0, (), jnp.float32),
    }


HIGH = lax.Precision.HIGHEST
full_turn = 2.0 * math.pi

def kept_freqs(count, cells):
    index = jnp.arange(count, dtype=jnp.int32)
    return jnp.where(index < count // 2, index, cells - count + index).astype(jnp.int32)

def phase_table(start, count, freqs, cells):
    places = start + jnp.arange(count, dtype=jnp.int32)
    product = places[:, None] * freqs[None, :] % cells
    angle = product.astype(jnp.float32) * (full_turn / cells)
    return (jnp.cos(angle), jnp.sin(angle))

def depth_table():
    cos_table, sin_table = phase_table(jnp.int32(0), GRID_Z, jnp.arange(MODES_Z, dtype=jnp.int32), GRID_Z)
    return jnp.concatenate([cos_table, -sin_table], axis=1)

def inverse_table():
    cos_table, sin_table = phase_table(jnp.int32(0), GRID_Z, jnp.arange(MODES_Z, dtype=jnp.int32), GRID_Z)
    weights = jnp.where(jnp.arange(MODES_Z) == 0, 1.0, 2.0).astype(jnp.float32)
    weights = weights * (0.5 / math.sqrt(MODES_X * MODES_Y * MODES_Z))
    return jnp.concatenate([(cos_table * weights).T, -(sin_table * weights).T], axis=0)

def rotate(real_part, imag_part, cos_table, sin_table, pattern, direction):
    contract = partial(jnp.einsum, pattern, precision=HIGH)
    new_real = contract(real_part, cos_table) + direction * contract(imag_part, sin_table)
    new_imag = contract(imag_part, cos_table) - direction * contract(real_part, sin_table)
    return (new_real, new_imag)

def mix_modes(spectrum, weight):
    contract = partial(jnp.einsum, 'bxycz,xycoz->bxyoz', precision=HIGH)
    spec_real, spec_imag = (spectrum[..., 0, :], spectrum[..., 1, :])
    weight_real, weight_imag = (weight[:, :, 0], weight[:, :, 1])
    out_real = contract(spec_real, weight_real) - contract(spec_imag, weight_imag)
    out_imag = contract(spec_real, weight_imag) + contract(spec_imag, weight_real)
    return jnp.stack([out_real, out_imag], axis=4)

def reference(field, spectral_weight, skip_weight, bias):
    block_rows = 16
    starts = (jnp.arange(GRID_X // block_rows, dtype=jnp.int32) * block_rows).astype(jnp.int32)
    table_z = depth_table().astype(jnp.bfloat16)
    forward_scale = (GRID_X * GRID_Y * GRID_Z) ** (-0.5)
    y_cos, y_sin = phase_table(jnp.int32(0), GRID_Y, kept_freqs(MODES_Y, GRID_Y), GRID_Y)

    def forward_block(carry, start):
        slab = lax.dynamic_slice_in_dim(field, start, block_rows, 2)
        depth_modes = jnp.dot(slab.reshape(-1, GRID_Z), table_z, preferred_element_type=jnp.float32)
        depth_modes = depth_modes.reshape(SLICES, CHANNELS, block_rows, GRID_Y, 2, MODES_Z)
        y_real, y_imag = rotate(depth_modes[..., 0, :], depth_modes[..., 1, :], y_cos * forward_scale, y_sin * forward_scale, 'bcxyk,ym->bxmck', 1.0)
        x_cos, x_sin = phase_table(start, block_rows, kept_freqs(MODES_X, GRID_X), GRID_X)
        x_real, x_imag = rotate(y_real, y_imag, x_cos, x_sin, 'bxyck,xm->bmyck', 1.0)
        return ((carry[0] + x_real, carry[1] + x_imag), None)
    empty = jnp.zeros((SLICES, MODES_X, MODES_Y, CHANNELS, MODES_Z), jnp.float32)
    (spec_real, spec_imag), _ = lax.scan(forward_block, (empty, empty), starts)
    spectrum = jnp.stack([spec_real, spec_imag], axis=4)
    mixed = mix_modes(spectrum, spectral_weight).astype(jnp.bfloat16)
    mixed = lax.optimization_barrier(mixed).astype(jnp.float32)
    table_back = inverse_table()
    skip_float = skip_weight.astype(jnp.float32)

    def inverse_block(start):
        x_cos, x_sin = phase_table(start, block_rows, kept_freqs(MODES_X, GRID_X), GRID_X)
        back_real, back_imag = rotate(mixed[..., 0, :], mixed[..., 1, :], x_cos, x_sin, 'bmnck,xm->bxnck', -1.0)
        full_real, full_imag = rotate(back_real, back_imag, y_cos, y_sin, 'bxnck,yn->bcxyk', -1.0)
        stacked = jnp.concatenate([full_real, full_imag], axis=-1).reshape(-1, 2 * MODES_Z)
        spectral = jnp.dot(stacked, table_back, precision=HIGH).reshape(SLICES, CHANNELS, block_rows, GRID_Y, GRID_Z)
        slab = lax.dynamic_slice_in_dim(field, start, block_rows, 2).astype(jnp.float32)
        skipped = jnp.einsum('oc,bcxyz->boxyz', skip_float, slab, precision=HIGH)
        total = spectral + skipped + bias[None, :, None, None, None]
        return jax.nn.gelu(total, approximate=False).astype(jnp.bfloat16)
    blocks = lax.map(inverse_block, starts)
    blocks = jnp.moveaxis(blocks, 0, 2)
    return blocks.reshape(SLICES, CHANNELS, GRID_X, GRID_Y, GRID_Z)
```

```python
import math

import jax
import jax.numpy as jnp
import numpy as np
from jax import lax
from jax.experimental import pallas as pl
from jax.experimental.pallas import tpu as pltpu
from jax.sharding import PartitionSpec as P

GRID = 256
CHANNELS = 16
MODES = 16
SLICES = 2
BLOCK = 16
RANK = 8
HALF = RANK * MODES
LANES = 2 * HALF
Z_CHIPS = 8
VMEM = 48 * 1024 * 1024
CENTRE = (BLOCK - 1) / 2


def make_tables():
    freq = np.concatenate([np.arange(8), np.arange(-8, 0)]).astype(np.float64)
    turn = 2.0 * np.pi / GRID
    u = np.arange(BLOCK) - CENTRE
    basis, weight = [], []
    for part in (np.cos(np.outer(u, turn * freq)), np.sin(np.outer(u, turn * freq))):
        left, scale, right = np.linalg.svd(part)
        basis.append(left[:, :4])
        weight.append(scale[:4, None] * right[:4])
    basis = np.concatenate(basis, axis=1)
    weight = np.concatenate(weight, axis=0)
    odd = np.arange(RANK) >= 4

    kz, z = np.arange(MODES), np.arange(GRID)
    angle = turn * np.outer(z, kz)
    depth = np.stack([np.cos(angle), -np.sin(angle)], axis=1)
    forward_z = np.repeat(depth[:, :, None, :], RANK, axis=2).reshape(GRID, LANES)
    w = np.where(kz == 0, 1.0, 2.0) * (0.5 / math.sqrt(MODES**3))
    inverse_z = np.repeat((depth * w)[:, :, None, :], RANK, axis=2).reshape(GRID, LANES).T
    lanes_x = np.tile(np.repeat(basis, MODES, axis=1), (1, 2))

    forward_y = np.zeros((16, 16, 2, 16, 16))
    inverse_y = np.zeros((16, 16, 2, 16, 16))
    scale = float(GRID) ** -1.5
    for q in range(16):
        for s in range(2):
            for chip in range(Z_CHIPS):
                theta = turn * freq[2 * chip + ((q % 2) ^ s)] * (16 * q + np.arange(16))
                row = s * Z_CHIPS + chip
                forward_y[q, row, 0] = (np.cos(theta) * scale)[None, :]
                forward_y[q, row, 1] = (np.sin(theta) * scale)[None, :]
                inverse_y[q, :, 0, row] = np.cos(theta)[:, None]
                inverse_y[q, :, 1, row] = -np.sin(theta)[:, None]

    phase = turn * np.outer(freq, 16 * np.arange(16) + CENTRE)
    forward_x = np.stack([np.cos(phase), np.sin(phase)], axis=1)
    forward_x = np.repeat(forward_x[..., None], CHANNELS, axis=3).reshape(16, 512)
    lanes_v = np.tile(np.repeat(weight.T, MODES, axis=1), (1, 2))
    inverse_x = np.zeros((16, 2, RANK, 2, MODES))
    for p in range(16):
        cos, sin = np.cos(phase[:, p]) * weight, np.sin(phase[:, p]) * weight
        real, imag = np.stack([cos, -sin], axis=1), np.stack([sin, cos], axis=1)
        turned = odd[:, None, None]
        inverse_x[p, 0] = np.where(turned, -imag, real)
        inverse_x[p, 1] = np.where(turned, real, imag)
    inverse_x = inverse_x.reshape(16, 16, 32)

    eye = np.eye(MODES)
    fold = np.zeros((2, RANK, MODES, 2, 8, MODES))
    for r in range(RANK):
        for a in range(2):
            if odd[r]:
                fold[a, r, :, 1 - a] = (1.0 if a else -1.0) * eye[:, None, :]
            else:
                fold[a, r, :, a] = eye[:, None, :]
    fold = fold.reshape(LANES, LANES)
    spread = np.zeros((RANK, 8, MODES, RANK, MODES))
    for r in range(RANK):
        spread[r, :, :, r, :] = eye[None]
    spread = spread.reshape(RANK * 128, 128)

    f32, bf16 = np.float32, jnp.bfloat16
    return dict(
        forward_z=forward_z.astype(f32),
        inverse_z=inverse_z.astype(f32).astype(bf16),
        lanes_x=lanes_x.astype(f32),
        forward_y=forward_y.reshape(16, 16, 512).astype(f32),
        inverse_y=inverse_y.reshape(16, 16, 512).astype(f32),
        forward_x=forward_x.astype(f32),
        lanes_v=lanes_v.astype(f32),
        inverse_x=inverse_x.astype(f32),
        fold=fold.astype(f32).astype(bf16),
        spread=spread.astype(f32).astype(bf16),
    )


def iota(shape, dim):
    return lax.broadcasted_iota(jnp.int32, shape, dim)


def dot(a, b):
    return jnp.dot(a, b, preferred_element_type=jnp.float32)


def repeat_rows(table):
    rows, lanes = table.shape
    return jnp.broadcast_to(table[:, None, :], (rows, 16, lanes)).reshape(rows * 16, lanes)


def tile_rows(table):
    rows, lanes = table.shape
    return jnp.broadcast_to(table[None], (16, rows, lanes)).reshape(rows * 16, lanes)


def masked(table, keep):
    return jnp.where(keep, table, 0.0).astype(jnp.bfloat16)


def turned(data):
    return jnp.concatenate([data[:, HALF:], -data[:, :HALF]], axis=1)


def with_turned(data):
    return jnp.concatenate([data, turned(data)], axis=0).astype(jnp.bfloat16)


def forward_kernel(
    index_ref, field_ref, weight_ref, table_z_ref, lanes_x_ref, table_y_ref,
    keep_ref, send_ref, packed_ref, held, total, arrived,
):
    def fetch(x):
        return pltpu.make_async_copy(field_ref.at[:, :, x], held.at[x], arrived.at[x])

    for x in range(BLOCK):
        fetch(x).start()

    place = (iota((MODES, LANES), 0) == iota((MODES, LANES), 1) % MODES).astype(jnp.bfloat16)
    wide = dot(weight_ref[...].astype(jnp.bfloat16), place)
    rows = iota((512, LANES), 0) % 16
    wide = masked(wide, rows == iota((512, LANES), 1) // MODES)
    gather = (iota((32, 512), 0) == iota((32, 512), 1) // 16).astype(jnp.bfloat16)
    packed_ref[...] = dot(gather, wide).astype(jnp.bfloat16)

    shape = (256, 512)
    table_y = masked(
        repeat_rows(table_y_ref[index_ref[0]]), iota(shape, 0) % 16 == iota(shape, 1) % 256 // 16
    )

    group = 4
    for start in range(0, BLOCK, group):
        for x in range(start, start + group):
            fetch(x).wait()
        data = jnp.concatenate(
            [held[x].reshape(SLICES * 256, GRID) for x in range(start, start + group)], axis=1
        )
        table = jnp.concatenate(
            [
                (table_z_ref[...] * lanes_x_ref[x : x + 1, :]).astype(jnp.bfloat16)
                for x in range(start, start + group)
            ],
            axis=0,
        )
        part = dot(data, table)
        total[...] = part if start == 0 else total[...] + part

    for b in range(SLICES):
        sums = dot(table_y, with_turned(total[b * 256 : (b + 1) * 256, :]))
        sums = sums.reshape(2, Z_CHIPS, CHANNELS, LANES)
        keep_ref[:, b] = sums[0]
        send_ref[:, b] = sums[1].astype(jnp.bfloat16)


def sum_kernel(parts_ref, packed_ref, out_ref):
    parts = parts_ref[...].astype(jnp.float32)
    sums = jnp.sum(parts, axis=0).reshape(32, LANES).astype(jnp.bfloat16)
    message = jnp.concatenate([sums, packed_ref[...]], axis=0)
    out_ref[...] = jnp.broadcast_to(message[None], out_ref.shape)


def mix_kernel(
    index_ref, got_ref, table_x_ref, lanes_v_ref, fold_ref, back_x_ref, spread_ref, out_ref,
):
    shape = (256, 512)
    table_x = masked(repeat_rows(table_x_ref[...]), iota(shape, 0) % 16 == iota(shape, 1) % 16)
    scale = repeat_rows(lanes_v_ref[...])
    mixed = []
    for b in range(SLICES):
        data = got_ref[:, b * 16 : (b + 1) * 16, :].reshape(256, LANES).astype(jnp.float32)
        modes = dot(table_x, with_turned(data)) * scale
        modes = dot(modes.astype(jnp.bfloat16), fold_ref[...]).reshape(MODES, CHANNELS, LANES)
        real, imag = modes[..., :HALF], modes[..., HALF:]
        for h in range(2):
            lanes = slice(h * HALF, (h + 1) * HALF)
            w_real = got_ref[:, 32:48, lanes].astype(jnp.float32)
            w_imag = got_ref[:, 48:64, lanes].astype(jnp.float32)
            out_real = jnp.sum(real * w_real - imag * w_imag, axis=1)
            out_imag = jnp.sum(real * w_imag + imag * w_real, axis=1)
            mixed.append(jnp.concatenate([out_real, out_imag], axis=0))
    mixed = jnp.concatenate(mixed, axis=1)
    mixed = mixed.astype(jnp.bfloat16).astype(jnp.float32)
    back = jnp.dot(
        back_x_ref[index_ref[0]], mixed, precision=lax.Precision.HIGHEST, preferred_element_type=jnp.float32
    )
    own = iota((8, 128), 0) == iota((8, 128), 1) // MODES
    rows = []
    for b in range(SLICES):
        for h in range(2):
            at = (2 * b + h) * 128
            for a in range(2):
                pieces = [
                    jnp.where(own, back[a * RANK + r : a * RANK + r + 1, at : at + 128], 0.0)
                    for r in range(RANK)
                ]
                rows.append(jnp.concatenate(pieces, axis=1))
    rows = jnp.concatenate(rows, axis=0).astype(jnp.bfloat16)
    rows = dot(rows, spread_ref[...]).reshape(SLICES, 2, 2, 8, HALF)
    for b in range(SLICES):
        half = [jnp.concatenate([rows[b, 0, a], rows[b, 1, a]], axis=0) for a in range(2)]
        message = jnp.concatenate(half, axis=1).astype(jnp.bfloat16)
        out_ref[:, b] = jnp.broadcast_to(message[None], (Z_CHIPS, CHANNELS, LANES))


def inverse_kernel(
    index_ref, field_ref, skip_ref, bias_ref, own_ref, other_ref, table_y_ref, table_z_ref, lanes_x_ref,
    out_ref, held, ready, left, bias, modes, arrived, sent,
):
    def fetch(x):
        return pltpu.make_async_copy(field_ref.at[:, :, x], held.at[x], arrived.at[x])

    def store(x):
        return pltpu.make_async_copy(ready.at[x], out_ref.at[:, :, x], sent.at[x])

    for x in range(BLOCK):
        fetch(x).start()

    shape = (256, 512)
    table_y = masked(
        tile_rows(table_y_ref[index_ref[0]]), iota(shape, 0) // 16 == iota(shape, 1) % 16
    )
    for b in range(SLICES):
        data = [ref[:, b].reshape(128, LANES) for ref in (own_ref, other_ref)]
        data = jnp.concatenate(data, axis=0).astype(jnp.float32)
        modes[b] = dot(table_y, with_turned(data))

    shape = (256, 256)
    place = (iota((16, 256), 0) == iota((16, 256), 1) // 16).astype(jnp.bfloat16)
    skip = repeat_rows(dot(skip_ref[...], place))
    left[...] = masked(skip, iota(shape, 0) % 16 == iota(shape, 1) % 16)
    one = iota((256, 16), 0) // 16 == iota((256, 16), 1)
    column = jnp.sum(jnp.where(one, bias_ref[...], 0.0), axis=1, keepdims=True)
    bias[...] = jnp.broadcast_to(column, bias.shape)

    def step(x, carry):
        fetch(x).wait()
        lanes = lanes_x_ref[pl.ds(x, 1), :]
        for b in range(SLICES):
            a = jnp.concatenate([left[...], (modes[b] * lanes).astype(jnp.bfloat16)], axis=1)
            c = jnp.concatenate([held[x, b].reshape(256, GRID), table_z_ref[...]], axis=0)
            value = dot(a, c) + bias[...]
            value = 0.5 * value * (1.0 + lax.erf(value * math.sqrt(0.5)))
            ready[x, b] = value.astype(jnp.bfloat16).reshape(CHANNELS, BLOCK, GRID)
        store(x).start()
        return carry

    lax.fori_loop(0, BLOCK, step, 0)
    for x in range(BLOCK):
        store(x).wait()


VM = pl.BlockSpec(memory_space=pltpu.VMEM)
SM = pl.BlockSpec(memory_space=pltpu.SMEM)
ANY = pl.BlockSpec(memory_space=pl.ANY)
PARAMS = pltpu.CompilerParams(vmem_limit_bytes=VMEM)
PAIR = [(i, i ^ 1) for i in range(16)]
CHIPS = [list(range(0, 16, 2)), list(range(1, 16, 2))]


def shape_of(shape, dtype):
    return jax.ShapeDtypeStruct(shape, dtype)


def on_device(field, spectral_weight, skip_weight, bias):
    t = make_tables()
    f32, bf16 = jnp.float32, jnp.bfloat16
    p = lax.axis_index("px").astype(jnp.int32).reshape(1)
    q = lax.axis_index("py").astype(jnp.int32).reshape(1)
    block = (SLICES, CHANNELS, BLOCK, GRID)
    part = (Z_CHIPS, SLICES, CHANNELS, LANES)

    keep, send, packed = pl.pallas_call(
        forward_kernel,
        name="forward",
        in_specs=[SM, ANY, VM, VM, VM, VM],
        out_specs=[VM, VM, VM],
        out_shape=[shape_of(part, f32), shape_of(part, bf16), shape_of((32, LANES), bf16)],
        scratch_shapes=[
            pltpu.VMEM((BLOCK, *block), bf16),
            pltpu.VMEM((512, LANES), f32),
            pltpu.SemaphoreType.DMA((BLOCK,)),
        ],
        compiler_params=PARAMS,
    )(q, field, spectral_weight.reshape(512, MODES), t["forward_z"], t["lanes_x"], t["forward_y"])
    got = lax.ppermute(send, "py", PAIR)
    sums = (keep + got.astype(f32)).astype(bf16)
    sums = lax.all_to_all(sums, "py", 0, 0, axis_index_groups=CHIPS, tiled=True)
    message = pl.pallas_call(
        sum_kernel,
        name="sum",
        in_specs=[VM, VM],
        out_specs=VM,
        out_shape=shape_of((16, 64, LANES), bf16),
        compiler_params=PARAMS,
    )(sums, packed)
    message = lax.all_to_all(message, "px", 0, 0, tiled=True)
    message = pl.pallas_call(
        mix_kernel,
        name="mix",
        in_specs=[SM, VM, VM, VM, VM, VM, VM],
        out_specs=VM,
        out_shape=shape_of(part, bf16),
        compiler_params=PARAMS,
    )(p, message, t["forward_x"], t["lanes_v"], t["fold"], t["inverse_x"], t["spread"])
    own = lax.all_to_all(message, "py", 0, 0, axis_index_groups=CHIPS, tiled=True)
    other = lax.ppermute(own, "py", PAIR)
    return pl.pallas_call(
        inverse_kernel,
        name="inverse",
        in_specs=[SM, ANY, VM, VM, VM, VM, VM, VM, VM],
        out_specs=ANY,
        out_shape=shape_of(field.shape, bf16),
        scratch_shapes=[
            pltpu.VMEM((BLOCK, *block), bf16),
            pltpu.VMEM((BLOCK, *block), bf16),
            pltpu.VMEM((256, 256), bf16),
            pltpu.VMEM((256, GRID), f32),
            pltpu.VMEM((SLICES, 256, LANES), f32),
            pltpu.SemaphoreType.DMA((BLOCK,)),
            pltpu.SemaphoreType.DMA((BLOCK,)),
        ],
        compiler_params=PARAMS,
    )(q, field, skip_weight, bias.reshape(1, 16), own, other, t["inverse_y"], t["inverse_z"], t["lanes_x"])


def solution(mesh):
    return jax.shard_map(
        on_device,
        mesh=mesh,
        in_specs=(P(None, None, "px", "py", None), P("px", "py", None, None, None, None), P(), P()),
        out_specs=P(None, None, "px", "py", None),
        check_vma=False,
    )
```

```python
import math

import jax
import jax.numpy as jnp
import numpy as np
from jax import lax
from jax.experimental import pallas as pl
from jax.experimental.pallas import tpu as pltpu
from jax.sharding import PartitionSpec as P

GRID = 256
CHANNELS = 16
MODES = 16
SLICES = 2
BLOCK = 16
RANK = 8
HALF = RANK * MODES
LANES = 2 * HALF
Z_CHIPS = 8
VMEM = 48 * 1024 * 1024
CENTRE = (BLOCK - 1) / 2


def make_tables():
    freq = np.concatenate([np.arange(8), np.arange(-8, 0)]).astype(np.float64)
    turn = 2.0 * np.pi / GRID
    u = np.arange(BLOCK) - CENTRE
    basis, weight = [], []
    for part in (np.cos(np.outer(u, turn * freq)), np.sin(np.outer(u, turn * freq))):
        left, scale, right = np.linalg.svd(part)
        basis.append(left[:, :4])
        weight.append(scale[:4, None] * right[:4])
    basis = np.concatenate(basis, axis=1)
    weight = np.concatenate(weight, axis=0)
    odd = np.arange(RANK) >= 4

    kz, z = np.arange(MODES), np.arange(GRID)
    angle = turn * np.outer(z, kz)
    depth = np.stack([np.cos(angle), -np.sin(angle)], axis=1)
    forward_z = np.repeat(depth[:, :, None, :], RANK, axis=2).reshape(GRID, LANES)
    w = np.where(kz == 0, 1.0, 2.0) * (0.5 / math.sqrt(MODES**3))
    inverse_z = np.zeros((4, 4, 2, MODES, GRID))
    for j in range(4):
        inverse_z[j, j] = (depth * w).transpose(1, 2, 0)
    inverse_z[:, :3, 1, 0] = 1.0
    inverse_z = inverse_z.reshape(4, 128, GRID)
    expand_x = np.einsum("xr,ab,kl->arkxbl", basis, np.eye(2), np.eye(MODES)).reshape(LANES, 512)
    lanes_x = np.tile(np.repeat(basis, MODES, axis=1), (1, 2))

    forward_y = np.zeros((16, 16, 2, 16, 16))
    inverse_y = np.zeros((16, 16, 2, 16, 16))
    scale = float(GRID) ** -1.5
    for q in range(16):
        for s in range(2):
            for chip in range(Z_CHIPS):
                theta = turn * freq[2 * chip + ((q % 2) ^ s)] * (16 * q + np.arange(16))
                row = s * Z_CHIPS + chip
                forward_y[q, row, 0] = (np.cos(theta) * scale)[None, :]
                forward_y[q, row, 1] = (np.sin(theta) * scale)[None, :]
                inverse_y[q, :, 0, row] = np.cos(theta)[:, None]
                inverse_y[q, :, 1, row] = -np.sin(theta)[:, None]

    phase = turn * np.outer(freq, 16 * np.arange(16) + CENTRE)
    forward_x = np.stack([np.cos(phase), np.sin(phase)], axis=1)
    forward_x = np.repeat(forward_x[..., None], CHANNELS, axis=3).reshape(16, 512)
    lanes_v = np.tile(np.repeat(weight.T, MODES, axis=1), (1, 2))
    inverse_x = np.zeros((16, 2, RANK, 2, MODES))
    for p in range(16):
        cos, sin = np.cos(phase[:, p]) * weight, np.sin(phase[:, p]) * weight
        real, imag = np.stack([cos, -sin], axis=1), np.stack([sin, cos], axis=1)
        turned = odd[:, None, None]
        inverse_x[p, 0] = np.where(turned, -imag, real)
        inverse_x[p, 1] = np.where(turned, real, imag)
    inverse_x = inverse_x.reshape(16, 16, 32)

    eye = np.eye(MODES)
    fold = np.zeros((2, RANK, MODES, 2, 8, MODES))
    for r in range(RANK):
        for a in range(2):
            if odd[r]:
                fold[a, r, :, 1 - a] = (1.0 if a else -1.0) * eye[:, None, :]
            else:
                fold[a, r, :, a] = eye[:, None, :]
    fold = fold.reshape(LANES, LANES)
    spread = np.zeros((RANK, 8, MODES, RANK, MODES))
    for r in range(RANK):
        spread[r, :, :, r, :] = eye[None]
    spread = spread.reshape(RANK * 128, 128)

    f32, bf16 = np.float32, jnp.bfloat16
    return dict(
        forward_z=forward_z.astype(f32),
        inverse_z=inverse_z.astype(f32).astype(bf16),
        expand_x=expand_x.astype(f32).astype(bf16),
        lanes_x=lanes_x.astype(f32),
        forward_y=forward_y.reshape(16, 16, 512).astype(f32),
        inverse_y=inverse_y.reshape(16, 16, 512).astype(f32),
        forward_x=forward_x.astype(f32),
        lanes_v=lanes_v.astype(f32),
        inverse_x=inverse_x.astype(f32),
        fold=fold.astype(f32).astype(bf16),
        spread=spread.astype(f32).astype(bf16),
    )


def iota(shape, dim):
    return lax.broadcasted_iota(jnp.int32, shape, dim)


def dot(a, b):
    return jnp.dot(a, b, preferred_element_type=jnp.float32)


def repeat_rows(table):
    rows, lanes = table.shape
    return jnp.broadcast_to(table[:, None, :], (rows, 16, lanes)).reshape(rows * 16, lanes)


def tile_rows(table):
    rows, lanes = table.shape
    return jnp.broadcast_to(table[None], (16, rows, lanes)).reshape(rows * 16, lanes)


def masked(table, keep):
    return jnp.where(keep, table, 0.0).astype(jnp.bfloat16)


def turned(data):
    return jnp.concatenate([data[:, HALF:], -data[:, :HALF]], axis=1)


def with_turned(data):
    return jnp.concatenate([data, turned(data)], axis=0).astype(jnp.bfloat16)


def forward_kernel(
    index_ref, field_hbm, weight_hbm, table_z_hbm, lanes_x_hbm, table_y_hbm,
    keep_ref, send_ref, packed_ref, held_ref,
    weight_ref, table_z_ref, lanes_x_ref, table_y_ref, total, arrived, loaded,
):
    small = [
        pltpu.make_async_copy(source, target, loaded.at[i])
        for i, (source, target) in enumerate(
            [
                (weight_hbm, weight_ref),
                (table_y_hbm.at[index_ref[0]], table_y_ref),
                (table_z_hbm, table_z_ref),
                (lanes_x_hbm, lanes_x_ref),
            ]
        )
    ]
    for copy in small:
        copy.start()

    def fetch(x):
        return pltpu.make_async_copy(field_hbm.at[:, :, x], held_ref.at[x], arrived.at[x])

    for x in range(BLOCK):
        fetch(x).start()

    place = (iota((MODES, LANES), 0) == iota((MODES, LANES), 1) % MODES).astype(jnp.bfloat16)
    rows = iota((512, LANES), 0) % 16
    gather = (iota((32, 512), 0) == iota((32, 512), 1) // 16).astype(jnp.bfloat16)
    small[0].wait()
    wide = dot(weight_ref[...].astype(jnp.bfloat16), place)
    wide = masked(wide, rows == iota((512, LANES), 1) // MODES)
    packed_ref[...] = dot(gather, wide).astype(jnp.bfloat16)

    shape = (256, 512)
    small[1].wait()
    table_y = masked(
        repeat_rows(table_y_ref[...]), iota(shape, 0) % 16 == iota(shape, 1) % 256 // 16
    )
    small[2].wait()
    small[3].wait()

    group = 4
    for start in range(0, BLOCK, group):
        table = jnp.concatenate(
            [
                (table_z_ref[...] * lanes_x_ref[x : x + 1, :]).astype(jnp.bfloat16)
                for x in range(start, start + group)
            ],
            axis=0,
        )
        for x in range(start, start + group):
            fetch(x).wait()
        data = jnp.concatenate(
            [held_ref[x].reshape(SLICES * 256, GRID) for x in range(start, start + group)], axis=1
        )
        part = dot(data, table)
        total[...] = part if start == 0 else total[...] + part

    for b in range(SLICES):
        sums = dot(table_y, with_turned(total[b * 256 : (b + 1) * 256, :]))
        sums = sums.reshape(2, Z_CHIPS, CHANNELS, LANES)
        keep_ref[:, b] = sums[0]
        send_ref[:, b] = sums[1].astype(jnp.bfloat16)


def sum_kernel(parts_ref, packed_ref, out_ref):
    parts = parts_ref[...].astype(jnp.float32)
    sums = jnp.sum(parts, axis=0).reshape(32, LANES).astype(jnp.bfloat16)
    message = jnp.concatenate([sums, packed_ref[...]], axis=0)
    out_ref[...] = jnp.broadcast_to(message[None], out_ref.shape)


def mix_kernel(
    index_ref, got_ref, table_x_ref, lanes_v_ref, fold_ref, back_x_ref, spread_ref, out_ref,
):
    shape = (256, 512)
    table_x = masked(repeat_rows(table_x_ref[...]), iota(shape, 0) % 16 == iota(shape, 1) % 16)
    scale = repeat_rows(lanes_v_ref[...])
    mixed = []
    for b in range(SLICES):
        data = got_ref[:, b * 16 : (b + 1) * 16, :].reshape(256, LANES).astype(jnp.float32)
        modes = dot(table_x, with_turned(data)) * scale
        modes = dot(modes.astype(jnp.bfloat16), fold_ref[...]).reshape(MODES, CHANNELS, LANES)
        real, imag = modes[..., :HALF], modes[..., HALF:]
        for h in range(2):
            lanes = slice(h * HALF, (h + 1) * HALF)
            w_real = got_ref[:, 32:48, lanes].astype(jnp.float32)
            w_imag = got_ref[:, 48:64, lanes].astype(jnp.float32)
            out_real = jnp.sum(real * w_real - imag * w_imag, axis=1)
            out_imag = jnp.sum(real * w_imag + imag * w_real, axis=1)
            mixed.append(jnp.concatenate([out_real, out_imag], axis=0))
    mixed = jnp.concatenate(mixed, axis=1)
    mixed = mixed.astype(jnp.bfloat16).astype(jnp.float32)
    back = jnp.dot(
        back_x_ref[index_ref[0]], mixed, precision=lax.Precision.HIGHEST, preferred_element_type=jnp.float32
    )
    own = iota((8, 128), 0) == iota((8, 128), 1) // MODES
    rows = []
    for b in range(SLICES):
        for h in range(2):
            at = (2 * b + h) * 128
            for a in range(2):
                pieces = [
                    jnp.where(own, back[a * RANK + r : a * RANK + r + 1, at : at + 128], 0.0)
                    for r in range(RANK)
                ]
                rows.append(jnp.concatenate(pieces, axis=1))
    rows = jnp.concatenate(rows, axis=0).astype(jnp.bfloat16)
    rows = dot(rows, spread_ref[...]).reshape(SLICES, 2, 2, 8, HALF)
    for b in range(SLICES):
        half = [jnp.concatenate([rows[b, 0, a], rows[b, 1, a]], axis=0) for a in range(2)]
        message = jnp.concatenate(half, axis=1).astype(jnp.bfloat16)
        out_ref[:, b] = jnp.broadcast_to(message[None], (Z_CHIPS, CHANNELS, LANES))


def inverse_kernel(
    index_ref, held_ref, skip_ref, bias_ref, own_ref, other_ref, table_y_ref, expand_ref, table_z_ref,
    out_ref, ready, sent,
):
    def store(x):
        return pltpu.make_async_copy(ready.at[x], out_ref.at[:, :, x], sent.at[x])

    shape = (256, 256)
    place = (iota((16, 256), 0) == iota((16, 256), 1) // 16).astype(jnp.bfloat16)
    skip = repeat_rows(dot(skip_ref[...], place))
    skip = masked(skip, iota(shape, 0) % 16 == iota(shape, 1) % 16)
    one = iota((256, 16), 0) // 16 == iota((256, 16), 1)
    bias = jnp.sum(jnp.where(one, bias_ref[...], 0.0), axis=1, keepdims=True)
    parts = []
    for _ in range(3):
        parts.append(bias.astype(jnp.bfloat16).astype(jnp.float32))
        bias = bias - parts[-1]

    shape = (256, 512)
    table_y = masked(
        tile_rows(table_y_ref[index_ref[0]]), iota(shape, 0) // 16 == iota(shape, 1) % 16
    )
    lane = iota(shape, 1) % 128
    modes = []
    for b in range(SLICES):
        data = [ref[:, b].reshape(128, LANES) for ref in (own_ref, other_ref)]
        data = jnp.concatenate(data, axis=0).astype(jnp.float32)
        rows = dot(table_y, with_turned(data)).astype(jnp.bfloat16)
        rows = dot(rows, expand_ref[...])
        for j in range(3):
            rows = jnp.where(lane == 32 * j + 16, parts[j], rows)
        modes.append(rows.astype(jnp.bfloat16))

    for x in range(BLOCK):
        at = x // 4 * 128
        for b in range(SLICES):
            value = dot(modes[b][:, at : at + 128], table_z_ref[x % 4])
            value = value + dot(skip, held_ref[x, b].reshape(256, GRID))
            half = 0.5 * value
            value = half + half * lax.erf(value * math.sqrt(0.5))
            ready[x, b] = value.astype(jnp.bfloat16).reshape(CHANNELS, BLOCK, GRID)
        store(x).start()
    for x in range(BLOCK):
        store(x).wait()


VM = pl.BlockSpec(memory_space=pltpu.VMEM)
SM = pl.BlockSpec(memory_space=pltpu.SMEM)
ANY = pl.BlockSpec(memory_space=pl.ANY)
PARAMS = pltpu.CompilerParams(vmem_limit_bytes=VMEM)
PAIR = [(i, i ^ 1) for i in range(16)]
CHIPS = [list(range(0, 16, 2)), list(range(1, 16, 2))]


def shape_of(shape, dtype):
    return jax.ShapeDtypeStruct(shape, dtype)


def on_device(field, spectral_weight, skip_weight, bias):
    t = make_tables()
    f32, bf16 = jnp.float32, jnp.bfloat16
    p = lax.axis_index("px").astype(jnp.int32).reshape(1)
    q = lax.axis_index("py").astype(jnp.int32).reshape(1)
    block = (SLICES, CHANNELS, BLOCK, GRID)
    part = (Z_CHIPS, SLICES, CHANNELS, LANES)

    far = [
        pltpu.with_memory_space_constraint(a, pltpu.HBM)
        for a in (
            field, spectral_weight.reshape(512, MODES), t["forward_z"], t["lanes_x"], t["forward_y"],
        )
    ]
    keep, send, packed, held = pl.pallas_call(
        forward_kernel,
        name="forward",
        in_specs=[SM, ANY, ANY, ANY, ANY, ANY],
        out_specs=[VM, VM, VM, VM],
        out_shape=[
            shape_of(part, f32),
            shape_of(part, bf16),
            shape_of((32, LANES), bf16),
            pltpu.VMEM((BLOCK, *block), bf16),
        ],
        scratch_shapes=[
            pltpu.VMEM((512, MODES), f32),
            pltpu.VMEM((GRID, LANES), f32),
            pltpu.VMEM((BLOCK, LANES), f32),
            pltpu.VMEM((16, 512), f32),
            pltpu.VMEM((512, LANES), f32),
            pltpu.SemaphoreType.DMA((BLOCK,)),
            pltpu.SemaphoreType.DMA((4,)),
        ],
        compiler_params=PARAMS,
    )(q, *far)
    got = lax.ppermute(send, "py", PAIR)
    sums = (keep + got.astype(f32)).astype(bf16)
    sums = lax.all_to_all(sums, "py", 0, 0, axis_index_groups=CHIPS, tiled=True)
    message = pl.pallas_call(
        sum_kernel,
        name="sum",
        in_specs=[VM, VM],
        out_specs=VM,
        out_shape=shape_of((16, 64, LANES), bf16),
        compiler_params=PARAMS,
    )(sums, packed)
    message = lax.all_to_all(message, "px", 0, 0, tiled=True)
    message = pl.pallas_call(
        mix_kernel,
        name="mix",
        in_specs=[SM, VM, VM, VM, VM, VM, VM],
        out_specs=VM,
        out_shape=shape_of(part, bf16),
        compiler_params=PARAMS,
    )(p, message, t["forward_x"], t["lanes_v"], t["fold"], t["inverse_x"], t["spread"])
    own = lax.all_to_all(message, "py", 0, 0, axis_index_groups=CHIPS, tiled=True)
    other = lax.ppermute(own, "py", PAIR)
    return pl.pallas_call(
        inverse_kernel,
        name="inverse",
        in_specs=[SM, VM, VM, VM, VM, VM, VM, VM, VM],
        out_specs=ANY,
        out_shape=shape_of(field.shape, bf16),
        scratch_shapes=[
            pltpu.VMEM((BLOCK, *block), bf16),
            pltpu.SemaphoreType.DMA((BLOCK,)),
        ],
        compiler_params=PARAMS,
    )(q, held, skip_weight, bias.reshape(1, 16), own, other, t["inverse_y"], t["expand_x"], t["inverse_z"])


def solution(mesh):
    return jax.shard_map(
        on_device,
        mesh=mesh,
        in_specs=(P(None, None, "px", "py", None), P("px", "py", None, None, None, None), P(), P()),
        out_specs=P(None, None, "px", "py", None),
        check_vma=False,
    )
```

```python
import math

import jax
import jax.numpy as jnp
import numpy as np
from jax import lax
from jax.experimental import pallas as pl
from jax.experimental.pallas import tpu as pltpu
from jax.sharding import PartitionSpec as P

GRID = 256
CHANNELS = 16
MODES = 16
SLICES = 2
BLOCK = 16
RANK = 8
EVEN = RANK // 2
HALF = RANK * MODES
LANES = 2 * HALF
Z_CHIPS = 8
GROUP = 4
GROUPS = BLOCK // GROUP
AHEAD = 3
VMEM = 24 * 1024 * 1024
CENTRE = (BLOCK - 1) / 2


def make_tables():
    freq = np.concatenate([np.arange(8), np.arange(-8, 0)]).astype(np.float64)
    turn = 2.0 * np.pi / GRID
    u = np.arange(BLOCK) - CENTRE
    basis, weight = [], []
    for part in (np.cos(np.outer(u, turn * freq)), np.sin(np.outer(u, turn * freq))):
        left, scale, right = np.linalg.svd(part)
        basis.append(left[:, :EVEN])
        weight.append(scale[:EVEN, None] * right[:EVEN])
    basis = np.concatenate(basis, axis=1)
    weight = np.concatenate(weight, axis=0)
    odd = np.arange(RANK) >= EVEN

    kz, z = np.arange(MODES), np.arange(GRID)
    angle = turn * np.outer(z, kz)
    depth = np.stack([np.cos(angle), -np.sin(angle)], axis=1)
    forward_z = np.repeat(depth[:, :, None, :], RANK, axis=2).reshape(GRID, LANES)
    w = np.where(kz == 0, 1.0, 2.0) * (0.5 / math.sqrt(MODES**3))
    inverse_z = (depth * w).transpose(1, 2, 0).reshape(2 * MODES, GRID)
    expand_x = np.einsum("xr,ab->arxb", basis, np.eye(2)).reshape(16, 32)
    expand_x = np.repeat(expand_x, MODES, axis=1)
    lanes_x = np.tile(np.repeat(basis, MODES, axis=1), (1, 2))

    forward_y = np.zeros((16, 16, 2, 16, 16))
    inverse_y = np.zeros((16, 16, 2, 16, 16))
    scale = float(GRID) ** -1.5
    for q in range(16):
        for s in range(2):
            for chip in range(Z_CHIPS):
                theta = turn * freq[2 * chip + ((q % 2) ^ s)] * (16 * q + np.arange(16))
                row = s * Z_CHIPS + chip
                forward_y[q, row, 0] = (np.cos(theta) * scale)[None, :]
                forward_y[q, row, 1] = (np.sin(theta) * scale)[None, :]
                inverse_y[q, :, 0, row] = np.cos(theta)[:, None]
                inverse_y[q, :, 1, row] = -np.sin(theta)[:, None]

    phase = turn * np.outer(freq, 16 * np.arange(16) + CENTRE)
    forward_x = np.stack([np.cos(phase), np.sin(phase)], axis=1)
    forward_x = np.repeat(forward_x[..., None], CHANNELS, axis=3).reshape(16, 512)
    lanes_v = np.tile(np.repeat(weight.T, MODES, axis=1), (1, 2))
    inverse_x = np.zeros((16, 2, RANK, 2, MODES))
    for p in range(16):
        cos, sin = np.cos(phase[:, p]) * weight, np.sin(phase[:, p]) * weight
        real, imag = np.stack([cos, -sin], axis=1), np.stack([sin, cos], axis=1)
        turned = odd[:, None, None]
        inverse_x[p, 0] = np.where(turned, -imag, real)
        inverse_x[p, 1] = np.where(turned, real, imag)
    inverse_x = inverse_x.reshape(16, 16, 32)

    tables = dict(
        forward_z=forward_z,
        inverse_z=inverse_z,
        expand_x=expand_x,
        lanes_x=lanes_x,
        forward_y=forward_y.reshape(16, 16, 512),
        inverse_y=inverse_y.reshape(16, 16, 512),
        forward_x=forward_x,
        lanes_v=lanes_v,
        inverse_x=inverse_x,
    )
    return {name: table.astype(np.float32) for name, table in tables.items()}


def iota(shape, dim):
    return lax.broadcasted_iota(jnp.int32, shape, dim)


def dot(a, b):
    return jnp.dot(a, b, preferred_element_type=jnp.float32)


def repeat_rows(table):
    rows, lanes = table.shape
    return jnp.broadcast_to(table[:, None, :], (rows, 16, lanes)).reshape(rows * 16, lanes)


def tile_rows(table):
    rows, lanes = table.shape
    return jnp.broadcast_to(table[None], (16, rows, lanes)).reshape(rows * 16, lanes)


def masked(table, keep):
    return jnp.where(keep, table, 0.0).astype(jnp.bfloat16)


def turned(data):
    return jnp.concatenate([data[:, HALF:], -data[:, :HALF]], axis=1)


def with_turned(data):
    return jnp.concatenate([data, turned(data)], axis=0).astype(jnp.bfloat16)


def forward_kernel(
    index_ref, field_hbm, weight_hbm, table_z_hbm, lanes_x_hbm, table_y_hbm, back_y_hbm, back_x_hbm,
    keep_ref, send_ref, packed_ref, back_y_ref, back_x_ref, first_ref, second_ref,
    rest, weight_ref, table_z_ref, lanes_x_ref, table_y_ref, total, arrived, loaded,
):
    small = [
        pltpu.make_async_copy(source, target, loaded.at[i])
        for i, (source, target) in enumerate(
            [
                (weight_hbm, weight_ref),
                (table_y_hbm.at[index_ref[1]], table_y_ref),
                (table_z_hbm, table_z_ref),
                (lanes_x_hbm, lanes_x_ref),
                (back_y_hbm.at[index_ref[1]], back_y_ref),
                (back_x_hbm.at[index_ref[0]], back_x_ref),
            ]
        )
    ]
    for copy in small:
        copy.start()
    held = [first_ref, second_ref, rest.at[0], rest.at[1]]

    def fetch(g):
        return pltpu.make_async_copy(field_hbm.at[:, :, pl.ds(g * GROUP, GROUP)], held[g], arrived.at[g])

    for g in range(AHEAD):
        fetch(g).start()

    place = (iota((MODES, LANES), 0) == iota((MODES, LANES), 1) % MODES).astype(jnp.bfloat16)
    rows = iota((512, LANES), 0) % 16
    gather = (iota((32, 512), 0) == iota((32, 512), 1) // 16).astype(jnp.bfloat16)
    small[0].wait()
    wide = dot(weight_ref[...].astype(jnp.bfloat16), place)
    wide = masked(wide, rows == iota((512, LANES), 1) // MODES)
    packed_ref[...] = dot(gather, wide).astype(jnp.bfloat16)

    shape = (256, 512)
    small[1].wait()
    table_y = masked(
        repeat_rows(table_y_ref[...]), iota(shape, 0) % 16 == iota(shape, 1) % 256 // 16
    )
    for copy in small[2:]:
        copy.wait()

    for g in range(GROUPS):
        table = jnp.concatenate(
            [
                (table_z_ref[...] * lanes_x_ref[x : x + 1, :]).astype(jnp.bfloat16)
                for x in range(g * GROUP, (g + 1) * GROUP)
            ],
            axis=0,
        )
        fetch(g).wait()
        if g + AHEAD < GROUPS:
            fetch(g + AHEAD).start()
        data = jnp.concatenate(
            [held[g][:, :, j].reshape(SLICES * 256, GRID) for j in range(GROUP)], axis=1
        )
        part = dot(data, table)
        total[...] = part if g == 0 else total[...] + part

    for b in range(SLICES):
        sums = dot(table_y, with_turned(total[b * 256 : (b + 1) * 256, :]))
        sums = sums.reshape(2, Z_CHIPS, CHANNELS, LANES)
        keep_ref[:, b] = sums[0]
        send_ref[:, b] = sums[1].astype(jnp.bfloat16)


def sum_kernel(parts_ref, packed_ref, out_ref):
    parts = parts_ref[...].astype(jnp.float32)
    sums = jnp.sum(parts, axis=0).reshape(32, LANES).astype(jnp.bfloat16)
    message = jnp.concatenate([sums, packed_ref[...]], axis=0)
    out_ref[...] = jnp.broadcast_to(message[None], out_ref.shape)


def mix_kernel(got_ref, table_x_ref, lanes_v_ref, back_x_ref, out_ref):
    shape = (LANES, LANES)
    row, lane = iota(shape, 0), iota(shape, 1)
    kind = jnp.where(row % HALF // MODES < EVEN, 0, 1)
    step = jnp.where(row < HALF, 0, 1) - jnp.where(lane < HALF, 0, 1)
    fold = jnp.where(kind == 0, jnp.where(step == 0, 1.0, 0.0), step.astype(jnp.float32))
    fold = masked(fold, row % MODES == lane % MODES)
    shape = (RANK * 128, 128)
    row, lane = iota(shape, 0), iota(shape, 1)
    spread = masked(jnp.where(row // 128 == lane // MODES, 1.0, 0.0), row % MODES == lane % MODES)

    shape = (256, 512)
    table_x = masked(repeat_rows(table_x_ref[...]), iota(shape, 0) % 16 == iota(shape, 1) % 16)
    scale = repeat_rows(lanes_v_ref[...])
    mixed = []
    for b in range(SLICES):
        data = got_ref[:, b * 16 : (b + 1) * 16, :].reshape(256, LANES).astype(jnp.float32)
        modes = dot(table_x, with_turned(data)) * scale
        modes = dot(modes.astype(jnp.bfloat16), fold).reshape(MODES, CHANNELS, LANES)
        real, imag = modes[..., :HALF], modes[..., HALF:]
        for h in range(2):
            lanes = slice(h * HALF, (h + 1) * HALF)
            w_real = got_ref[:, 32:48, lanes].astype(jnp.float32)
            w_imag = got_ref[:, 48:64, lanes].astype(jnp.float32)
            out_real = jnp.sum(real * w_real - imag * w_imag, axis=1)
            out_imag = jnp.sum(real * w_imag + imag * w_real, axis=1)
            mixed.append(jnp.concatenate([out_real, out_imag], axis=0))
    mixed = jnp.concatenate(mixed, axis=1)
    mixed = mixed.astype(jnp.bfloat16).astype(jnp.float32)
    back = jnp.dot(
        back_x_ref[...], mixed, precision=lax.Precision.HIGHEST, preferred_element_type=jnp.float32
    )
    own = iota((8, 128), 0) == iota((8, 128), 1) // MODES
    rows = []
    for b in range(SLICES):
        for h in range(2):
            at = (2 * b + h) * 128
            for a in range(2):
                pieces = [
                    jnp.where(own, back[a * RANK + r : a * RANK + r + 1, at : at + 128], 0.0)
                    for r in range(RANK)
                ]
                rows.append(jnp.concatenate(pieces, axis=1))
    rows = jnp.concatenate(rows, axis=0).astype(jnp.bfloat16)
    rows = dot(rows, spread).reshape(SLICES, 2, 2, 8, HALF)
    for b in range(SLICES):
        half = [jnp.concatenate([rows[b, 0, a], rows[b, 1, a]], axis=0) for a in range(2)]
        message = jnp.concatenate(half, axis=1).astype(jnp.bfloat16)
        out_ref[:, b] = jnp.broadcast_to(message[None], (Z_CHIPS, CHANNELS, LANES))


def inverse_kernel(
    field_hbm, first_ref, second_ref, skip_ref, bias_ref, own_ref, other_ref,
    table_y_ref, expand_ref, table_z_ref,
    out_ref, rest, ready, arrived, sent,
):
    held = [first_ref, second_ref, rest.at[0], rest.at[1]]

    def fetch(g):
        return pltpu.make_async_copy(field_hbm.at[:, :, pl.ds(g * GROUP, GROUP)], held[g], arrived.at[g - 2])

    def store(g):
        return pltpu.make_async_copy(ready.at[g], out_ref.at[:, :, pl.ds(g * GROUP, GROUP)], sent.at[g])

    for g in (2, 3):
        fetch(g).start()

    shape = (256, 256)
    place = (iota((16, 256), 0) == iota((16, 256), 1) // 16).astype(jnp.bfloat16)
    skip = repeat_rows(dot(skip_ref[...], place))
    skip = masked(skip, iota(shape, 0) % 16 == iota(shape, 1) % 16)
    one = iota((256, 16), 0) // 16 == iota((256, 16), 1)
    bias = jnp.sum(jnp.where(one, bias_ref[...], 0.0), axis=1, keepdims=True)
    parts = []
    for _ in range(3):
        parts.append(bias.astype(jnp.bfloat16).astype(jnp.float32))
        bias = bias - parts[-1]

    shape = (2 * MODES, GRID)
    ones = jnp.where(iota(shape, 0) == MODES, 1.0, 0.0)
    tables_z = []
    for j in range(GROUP):
        blocks = [ones, ones, ones, jnp.zeros(shape, jnp.float32)]
        blocks[j] = blocks[j] + table_z_ref[...]
        tables_z.append(jnp.concatenate(blocks, axis=0).astype(jnp.bfloat16))

    shape = (256, 512)
    table_y = masked(tile_rows(table_y_ref[...]), iota(shape, 0) // 16 == iota(shape, 1) % 16)
    expand = masked(repeat_rows(expand_ref[...]), iota(shape, 0) % 16 == iota(shape, 1) % 16)
    lane = iota(shape, 1) % 128
    modes = []
    for b in range(SLICES):
        data = [ref[:, b].reshape(128, LANES) for ref in (own_ref, other_ref)]
        data = jnp.concatenate(data, axis=0).astype(jnp.float32)
        rows = dot(table_y, with_turned(data)).astype(jnp.bfloat16)
        rows = dot(rows, expand)
        for j in range(3):
            rows = jnp.where(lane == 32 * j + 16, parts[j], rows)
        modes.append(rows.astype(jnp.bfloat16))

    for g in range(GROUPS):
        if g >= 2:
            fetch(g).wait()
        for j in range(GROUP):
            for b in range(SLICES):
                value = dot(modes[b][:, g * 128 : (g + 1) * 128], tables_z[j])
                value = value + dot(skip, held[g][b, :, j].reshape(256, GRID))
                half = 0.5 * value
                value = half + half * lax.erf(value * math.sqrt(0.5))
                ready[g, b, :, j] = value.astype(jnp.bfloat16).reshape(CHANNELS, BLOCK, GRID)
        store(g).start()
    for g in range(GROUPS):
        store(g).wait()


VM = pl.BlockSpec(memory_space=pltpu.VMEM)
SM = pl.BlockSpec(memory_space=pltpu.SMEM)
ANY = pl.BlockSpec(memory_space=pl.ANY)
PARAMS = pltpu.CompilerParams(vmem_limit_bytes=VMEM)
PAIR = [(i, i ^ 1) for i in range(16)]
CHIPS = [list(range(0, 16, 2)), list(range(1, 16, 2))]


def shape_of(shape, dtype):
    return jax.ShapeDtypeStruct(shape, dtype)


def on_device(field, spectral_weight, skip_weight, bias):
    t = make_tables()
    f32, bf16 = jnp.float32, jnp.bfloat16
    place = jnp.stack([lax.axis_index("px"), lax.axis_index("py")]).astype(jnp.int32)
    planes = (SLICES, CHANNELS, GROUP, BLOCK, GRID)
    part = (Z_CHIPS, SLICES, CHANNELS, LANES)

    far = [
        pltpu.with_memory_space_constraint(a, pltpu.HBM)
        for a in (
            field, spectral_weight.reshape(512, MODES), t["forward_z"], t["lanes_x"], t["forward_y"],
            t["inverse_y"], t["inverse_x"],
        )
    ]
    keep, send, packed, back_y, back_x, *held = pl.pallas_call(
        forward_kernel,
        name="forward",
        in_specs=[SM] + [ANY] * 7,
        out_specs=[VM] * 7,
        out_shape=[
            shape_of(part, f32),
            shape_of(part, bf16),
            shape_of((32, LANES), bf16),
            shape_of((16, 512), f32),
            shape_of((16, 32), f32),
            pltpu.VMEM(planes, bf16),
            pltpu.VMEM(planes, bf16),
        ],
        scratch_shapes=[
            pltpu.VMEM((2, *planes), bf16),
            pltpu.VMEM((512, MODES), f32),
            pltpu.VMEM((GRID, LANES), f32),
            pltpu.VMEM((BLOCK, LANES), f32),
            pltpu.VMEM((16, 512), f32),
            pltpu.VMEM((512, LANES), f32),
            pltpu.SemaphoreType.DMA((GROUPS,)),
            pltpu.SemaphoreType.DMA((6,)),
        ],
        compiler_params=PARAMS,
    )(place, *far)
    got = lax.ppermute(send, "py", PAIR)
    sums = (keep + got.astype(f32)).astype(bf16)
    sums = lax.all_to_all(sums, "py", 0, 0, axis_index_groups=CHIPS, tiled=True)
    message = pl.pallas_call(
        sum_kernel,
        name="sum",
        in_specs=[VM, VM],
        out_specs=VM,
        out_shape=shape_of((16, 64, LANES), bf16),
        compiler_params=PARAMS,
    )(sums, packed)
    message = lax.all_to_all(message, "px", 0, 0, tiled=True)
    message = pl.pallas_call(
        mix_kernel,
        name="mix",
        in_specs=[VM, VM, VM, VM],
        out_specs=VM,
        out_shape=shape_of(part, bf16),
        compiler_params=PARAMS,
    )(message, t["forward_x"], t["lanes_v"], back_x)
    own = lax.all_to_all(message, "py", 0, 0, axis_index_groups=CHIPS, tiled=True)
    other = lax.ppermute(own, "py", PAIR)
    return pl.pallas_call(
        inverse_kernel,
        name="inverse",
        in_specs=[ANY] + [VM] * 9,
        out_specs=ANY,
        out_shape=shape_of(field.shape, bf16),
        scratch_shapes=[
            pltpu.VMEM((2, *planes), bf16),
            pltpu.VMEM((GROUPS, *planes), bf16),
            pltpu.SemaphoreType.DMA((2,)),
            pltpu.SemaphoreType.DMA((GROUPS,)),
        ],
        compiler_params=PARAMS,
    )(far[0], *held, skip_weight, bias.reshape(1, 16), own, other, back_y, t["expand_x"], t["inverse_z"])


def solution(mesh):
    return jax.shard_map(
        on_device,
        mesh=mesh,
        in_specs=(P(None, None, "px", "py", None), P("px", "py", None, None, None, None), P(), P()),
        out_specs=P(None, None, "px", "py", None),
        check_vma=False,
    )
```

```python
import math

import jax
import jax.numpy as jnp
import numpy as np
from jax import lax
from jax.experimental import pallas as pl
from jax.experimental.pallas import tpu as pltpu
from jax.sharding import PartitionSpec as P

GRID = 256
CHANNELS = 16
MODES = 16
SLICES = 2
BLOCK = 16
RANK = 8
EVEN = RANK // 2
HALF = RANK * MODES
LANES = 2 * HALF
Z_CHIPS = 8
GROUP = 4
GROUPS = BLOCK // GROUP
AHEAD = 3
ROWS = 128
VMEM = 24 * 1024 * 1024
CENTRE = (BLOCK - 1) / 2


def make_tables():
    freq = np.concatenate([np.arange(8), np.arange(-8, 0)]).astype(np.float64)
    turn = 2.0 * np.pi / GRID
    u = np.arange(BLOCK) - CENTRE
    basis, weight = [], []
    for part in (np.cos(np.outer(u, turn * freq)), np.sin(np.outer(u, turn * freq))):
        left, scale, right = np.linalg.svd(part)
        basis.append(left[:, :EVEN])
        weight.append(scale[:EVEN, None] * right[:EVEN])
    basis = np.concatenate(basis, axis=1)
    weight = np.concatenate(weight, axis=0)
    odd = np.arange(RANK) >= EVEN

    kz, z = np.arange(MODES), np.arange(GRID)
    angle = turn * np.outer(z, kz)
    depth = np.stack([np.cos(angle), -np.sin(angle)], axis=1)
    forward_z = np.repeat(depth[:, :, None, :], RANK, axis=2).reshape(GRID, LANES)
    w = np.where(kz == 0, 1.0, 2.0) * (0.5 / math.sqrt(MODES**3))
    inverse_z = (depth * w).transpose(1, 2, 0).reshape(2 * MODES, GRID)
    expand_x = np.einsum("xr,ab->arxb", basis, np.eye(2)).reshape(16, 32)
    expand_x = np.repeat(expand_x, MODES, axis=1)
    lanes_x = np.tile(np.repeat(basis, MODES, axis=1), (1, 2))

    forward_y = np.zeros((16, 16, 2, 16, 16))
    inverse_y = np.zeros((16, 16, 2, 16, 16))
    scale = float(GRID) ** -1.5
    for q in range(16):
        for s in range(2):
            for chip in range(Z_CHIPS):
                theta = turn * freq[2 * chip + ((q % 2) ^ s)] * (16 * q + np.arange(16))
                row = s * Z_CHIPS + chip
                forward_y[q, row, 0] = (np.cos(theta) * scale)[None, :]
                forward_y[q, row, 1] = (np.sin(theta) * scale)[None, :]
                inverse_y[q, :, 0, row] = np.cos(theta)[:, None]
                inverse_y[q, :, 1, row] = -np.sin(theta)[:, None]

    phase = turn * np.outer(freq, 16 * np.arange(16) + CENTRE)
    forward_x = np.stack([np.cos(phase), np.sin(phase)], axis=1)
    forward_x = np.repeat(forward_x[..., None], CHANNELS, axis=3).reshape(16, 512)
    lanes_v = np.tile(np.repeat(weight.T, MODES, axis=1), (1, 2))
    inverse_x = np.zeros((16, 2, RANK, 2, MODES))
    for p in range(16):
        cos, sin = np.cos(phase[:, p]) * weight, np.sin(phase[:, p]) * weight
        real, imag = np.stack([cos, -sin], axis=1), np.stack([sin, cos], axis=1)
        turned = odd[:, None, None]
        inverse_x[p, 0] = np.where(turned, -imag, real)
        inverse_x[p, 1] = np.where(turned, real, imag)
    inverse_x = inverse_x.reshape(16, 16, 32)

    tables = dict(
        forward_z=forward_z,
        inverse_z=inverse_z,
        expand_x=expand_x,
        lanes_x=lanes_x,
        forward_y=forward_y.reshape(16, 16, 512),
        inverse_y=inverse_y.reshape(16, 16, 512),
        forward_x=forward_x,
        lanes_v=lanes_v,
        inverse_x=inverse_x,
    )
    return {name: table.astype(np.float32) for name, table in tables.items()}


def iota(shape, dim):
    return lax.broadcasted_iota(jnp.int32, shape, dim)


def dot(a, b):
    return jnp.dot(a, b, preferred_element_type=jnp.float32)


def repeat_rows(table):
    rows, lanes = table.shape
    return jnp.broadcast_to(table[:, None, :], (rows, 16, lanes)).reshape(rows * 16, lanes)


def tile_rows(table):
    rows, lanes = table.shape
    return jnp.broadcast_to(table[None], (16, rows, lanes)).reshape(rows * 16, lanes)


def masked(table, keep):
    return jnp.where(keep, table, 0.0).astype(jnp.bfloat16)


def turned(data):
    return jnp.concatenate([data[:, HALF:], -data[:, :HALF]], axis=1)


def with_turned(data):
    return jnp.concatenate([data, turned(data)], axis=0).astype(jnp.bfloat16)


def forward_kernel(
    index_ref, field_hbm, weight_hbm, table_z_hbm, lanes_x_hbm, table_y_hbm, back_y_hbm, back_x_hbm,
    keep_ref, send_ref, packed_ref, back_y_ref, back_x_ref, first_ref, second_ref,
    rest, weight_ref, table_z_ref, lanes_x_ref, table_y_ref, total, arrived, loaded,
):
    small = [
        pltpu.make_async_copy(source, target, loaded.at[i])
        for i, (source, target) in enumerate(
            [
                (weight_hbm, weight_ref),
                (table_y_hbm.at[index_ref[1]], table_y_ref),
                (table_z_hbm, table_z_ref),
                (lanes_x_hbm, lanes_x_ref),
                (back_y_hbm.at[index_ref[1]], back_y_ref),
                (back_x_hbm.at[index_ref[0]], back_x_ref),
            ]
        )
    ]
    for copy in small:
        copy.start()
    held = [first_ref, second_ref, rest.at[0], rest.at[1]]

    def fetch(g):
        return pltpu.make_async_copy(field_hbm.at[:, :, pl.ds(g * GROUP, GROUP)], held[g], arrived.at[g])

    for g in range(AHEAD):
        fetch(g).start()

    place = (iota((MODES, LANES), 0) == iota((MODES, LANES), 1) % MODES).astype(jnp.bfloat16)
    rows = iota((512, LANES), 0) % 16
    gather = (iota((32, 512), 0) == iota((32, 512), 1) // 16).astype(jnp.bfloat16)
    small[0].wait()
    wide = dot(weight_ref[...].astype(jnp.bfloat16), place)
    wide = masked(wide, rows == iota((512, LANES), 1) // MODES)
    packed_ref[...] = dot(gather, wide).astype(jnp.bfloat16)

    shape = (256, 512)
    small[1].wait()
    table_y = masked(
        repeat_rows(table_y_ref[...]), iota(shape, 0) % 16 == iota(shape, 1) % 256 // 16
    )
    for copy in small[2:]:
        copy.wait()

    for g in range(GROUPS):
        table = jnp.concatenate(
            [
                (table_z_ref[...] * lanes_x_ref[x : x + 1, :]).astype(jnp.bfloat16)
                for x in range(g * GROUP, (g + 1) * GROUP)
            ],
            axis=0,
        )
        fetch(g).wait()
        if g + AHEAD < GROUPS:
            fetch(g + AHEAD).start()
        data = jnp.concatenate(
            [held[g][:, :, j].reshape(SLICES * 256, GRID) for j in range(GROUP)], axis=1
        )
        part = dot(data, table)
        total[...] = part if g == 0 else total[...] + part

    for b in range(SLICES):
        sums = dot(table_y, with_turned(total[b * 256 : (b + 1) * 256, :]))
        sums = sums.reshape(2, Z_CHIPS, CHANNELS, LANES)
        keep_ref[:, b] = sums[0]
        send_ref[:, b] = sums[1].astype(jnp.bfloat16)


def sum_kernel(parts_ref, packed_ref, out_ref):
    parts = parts_ref[...].astype(jnp.float32)
    sums = jnp.sum(parts, axis=0).reshape(32, LANES).astype(jnp.bfloat16)
    message = jnp.concatenate([sums, packed_ref[...]], axis=0)
    out_ref[...] = jnp.broadcast_to(message[None], out_ref.shape)


def mix_kernel(got_ref, table_x_ref, lanes_v_ref, back_x_ref, out_ref):
    shape = (LANES, LANES)
    row, lane = iota(shape, 0), iota(shape, 1)
    kind = jnp.where(row % HALF // MODES < EVEN, 0, 1)
    step = jnp.where(row < HALF, 0, 1) - jnp.where(lane < HALF, 0, 1)
    fold = jnp.where(kind == 0, jnp.where(step == 0, 1.0, 0.0), step.astype(jnp.float32))
    fold = masked(fold, row % MODES == lane % MODES)
    shape = (RANK * 128, 128)
    row, lane = iota(shape, 0), iota(shape, 1)
    spread = masked(jnp.where(row // 128 == lane // MODES, 1.0, 0.0), row % MODES == lane % MODES)

    shape = (256, 512)
    table_x = masked(repeat_rows(table_x_ref[...]), iota(shape, 0) % 16 == iota(shape, 1) % 16)
    scale = repeat_rows(lanes_v_ref[...])
    mixed = []
    for b in range(SLICES):
        data = got_ref[:, b * 16 : (b + 1) * 16, :].reshape(256, LANES).astype(jnp.float32)
        modes = dot(table_x, with_turned(data)) * scale
        modes = dot(modes.astype(jnp.bfloat16), fold).reshape(MODES, CHANNELS, LANES)
        real, imag = modes[..., :HALF], modes[..., HALF:]
        for h in range(2):
            lanes = slice(h * HALF, (h + 1) * HALF)
            w_real = got_ref[:, 32:48, lanes].astype(jnp.float32)
            w_imag = got_ref[:, 48:64, lanes].astype(jnp.float32)
            out_real = jnp.sum(real * w_real - imag * w_imag, axis=1)
            out_imag = jnp.sum(real * w_imag + imag * w_real, axis=1)
            mixed.append(jnp.concatenate([out_real, out_imag], axis=0))
    mixed = jnp.concatenate(mixed, axis=1)
    mixed = mixed.astype(jnp.bfloat16).astype(jnp.float32)
    back = jnp.dot(
        back_x_ref[...], mixed, precision=lax.Precision.HIGHEST, preferred_element_type=jnp.float32
    )
    own = iota((8, 128), 0) == iota((8, 128), 1) // MODES
    rows = []
    for b in range(SLICES):
        for h in range(2):
            at = (2 * b + h) * 128
            for a in range(2):
                pieces = [
                    jnp.where(own, back[a * RANK + r : a * RANK + r + 1, at : at + 128], 0.0)
                    for r in range(RANK)
                ]
                rows.append(jnp.concatenate(pieces, axis=1))
    rows = jnp.concatenate(rows, axis=0).astype(jnp.bfloat16)
    rows = dot(rows, spread).reshape(SLICES, 2, 2, 8, HALF)
    for b in range(SLICES):
        half = [jnp.concatenate([rows[b, 0, a], rows[b, 1, a]], axis=0) for a in range(2)]
        message = jnp.concatenate(half, axis=1).astype(jnp.bfloat16)
        out_ref[:, b] = jnp.broadcast_to(message[None], (Z_CHIPS, CHANNELS, LANES))


def inverse_kernel(
    field_hbm, first_ref, second_ref, skip_ref, bias_ref, own_ref, other_ref,
    table_y_ref, expand_ref, table_z_ref,
    out_ref, rest, ready, arrived, sent,
):
    held = [first_ref, second_ref, rest.at[0], rest.at[1]]

    def fetch(g):
        return pltpu.make_async_copy(field_hbm.at[:, :, pl.ds(g * GROUP, GROUP)], held[g], arrived.at[g - 2])

    def store(g, j, count):
        return pltpu.make_async_copy(
            ready.at[g, :, :, pl.ds(j, count)],
            out_ref.at[:, :, pl.ds(g * GROUP + j, count)],
            sent.at[g + j // 2],
        )

    for g in (2, 3):
        fetch(g).start()

    shape = (256, 256)
    place = (iota((16, 256), 0) == iota((16, 256), 1) // 16).astype(jnp.bfloat16)
    skip = repeat_rows(dot(skip_ref[...], place))
    skip = masked(skip, iota(shape, 0) % 16 == iota(shape, 1) % 16)
    one = iota((256, 16), 0) // 16 == iota((256, 16), 1)
    bias = jnp.sum(jnp.where(one, bias_ref[...], 0.0), axis=1, keepdims=True)
    parts = []
    for _ in range(3):
        parts.append(bias.astype(jnp.bfloat16).astype(jnp.float32))
        bias = bias - parts[-1]

    shape = (2 * MODES, GRID)
    ones = jnp.where(iota(shape, 0) == MODES, 1.0, 0.0)
    tables_z = []
    for j in range(GROUP):
        blocks = [ones, ones, ones, jnp.zeros(shape, jnp.float32)]
        blocks[j] = blocks[j] + table_z_ref[...]
        tables_z.append(jnp.concatenate(blocks, axis=0).astype(jnp.bfloat16))

    shape = (256, 512)
    table_y = masked(tile_rows(table_y_ref[...]), iota(shape, 0) // 16 == iota(shape, 1) % 16)
    expand = masked(repeat_rows(expand_ref[...]), iota(shape, 0) % 16 == iota(shape, 1) % 16)
    lane = iota(shape, 1) % 128
    modes = []
    for b in range(SLICES):
        data = [ref[:, b].reshape(128, LANES) for ref in (own_ref, other_ref)]
        data = jnp.concatenate(data, axis=0).astype(jnp.float32)
        rows = dot(table_y, with_turned(data)).astype(jnp.bfloat16)
        rows = dot(rows, expand)
        for j in range(3):
            rows = jnp.where(lane == 32 * j + 16, parts[j], rows)
        modes.append(rows.astype(jnp.bfloat16))

    stores = []
    for g in range(GROUPS):
        if g >= 2:
            fetch(g).wait()
        for j in range(GROUP):
            for b in range(SLICES):
                lhs = modes[b][:, g * 128 : (g + 1) * 128]
                for r in range(0, 256, ROWS):
                    value = dot(lhs[r : r + ROWS], tables_z[j])
                    value = value + dot(skip[r : r + ROWS], held[g][b, :, j].reshape(256, GRID))
                    half = 0.5 * value
                    value = half + half * lax.erf(value * math.sqrt(0.5))
                    value = value.astype(jnp.bfloat16).reshape(ROWS // BLOCK, BLOCK, GRID)
                    ready[g, b, r // BLOCK : (r + ROWS) // BLOCK, j] = value
            if g == GROUPS - 1 and j % 2 == 1:
                stores.append(store(g, j - 1, 2))
            elif g < GROUPS - 1 and j == GROUP - 1:
                stores.append(store(g, 0, GROUP))
            else:
                continue
            stores[-1].start()
    for copy in stores:
        copy.wait()


VM = pl.BlockSpec(memory_space=pltpu.VMEM)
SM = pl.BlockSpec(memory_space=pltpu.SMEM)
ANY = pl.BlockSpec(memory_space=pl.ANY)
PARAMS = pltpu.CompilerParams(vmem_limit_bytes=VMEM)
PAIR = [(i, i ^ 1) for i in range(16)]
CHIPS = [list(range(0, 16, 2)), list(range(1, 16, 2))]


def shape_of(shape, dtype):
    return jax.ShapeDtypeStruct(shape, dtype)


def on_device(field, spectral_weight, skip_weight, bias):
    t = make_tables()
    f32, bf16 = jnp.float32, jnp.bfloat16
    place = jnp.stack([lax.axis_index("px"), lax.axis_index("py")]).astype(jnp.int32)
    planes = (SLICES, CHANNELS, GROUP, BLOCK, GRID)
    part = (Z_CHIPS, SLICES, CHANNELS, LANES)

    far = [
        pltpu.with_memory_space_constraint(a, pltpu.HBM)
        for a in (
            field, spectral_weight.reshape(512, MODES), t["forward_z"], t["lanes_x"], t["forward_y"],
            t["inverse_y"], t["inverse_x"],
        )
    ]
    keep, send, packed, back_y, back_x, *held = pl.pallas_call(
        forward_kernel,
        name="forward",
        in_specs=[SM] + [ANY] * 7,
        out_specs=[VM] * 7,
        out_shape=[
            shape_of(part, f32),
            shape_of(part, bf16),
            shape_of((32, LANES), bf16),
            shape_of((16, 512), f32),
            shape_of((16, 32), f32),
            pltpu.VMEM(planes, bf16),
            pltpu.VMEM(planes, bf16),
        ],
        scratch_shapes=[
            pltpu.VMEM((2, *planes), bf16),
            pltpu.VMEM((512, MODES), f32),
            pltpu.VMEM((GRID, LANES), f32),
            pltpu.VMEM((BLOCK, LANES), f32),
            pltpu.VMEM((16, 512), f32),
            pltpu.VMEM((512, LANES), f32),
            pltpu.SemaphoreType.DMA((GROUPS,)),
            pltpu.SemaphoreType.DMA((6,)),
        ],
        compiler_params=PARAMS,
    )(place, *far)
    got = lax.ppermute(send, "py", PAIR)
    sums = (keep + got.astype(f32)).astype(bf16)
    sums = lax.all_to_all(sums, "py", 0, 0, axis_index_groups=CHIPS, tiled=True)
    message = pl.pallas_call(
        sum_kernel,
        name="sum",
        in_specs=[VM, VM],
        out_specs=VM,
        out_shape=shape_of((16, 64, LANES), bf16),
        compiler_params=PARAMS,
    )(sums, packed)
    message = lax.all_to_all(message, "px", 0, 0, tiled=True)
    message = pl.pallas_call(
        mix_kernel,
        name="mix",
        in_specs=[VM, VM, VM, VM],
        out_specs=VM,
        out_shape=shape_of(part, bf16),
        compiler_params=PARAMS,
    )(message, t["forward_x"], t["lanes_v"], back_x)
    own = lax.all_to_all(message, "py", 0, 0, axis_index_groups=CHIPS, tiled=True)
    other = lax.ppermute(own, "py", PAIR)
    return pl.pallas_call(
        inverse_kernel,
        name="inverse",
        in_specs=[ANY] + [VM] * 9,
        out_specs=ANY,
        out_shape=shape_of(field.shape, bf16),
        scratch_shapes=[
            pltpu.VMEM((2, *planes), bf16),
            pltpu.VMEM((GROUPS, *planes), bf16),
            pltpu.SemaphoreType.DMA((2,)),
            pltpu.SemaphoreType.DMA((GROUPS + 1,)),
        ],
        compiler_params=PARAMS,
    )(far[0], *held, skip_weight, bias.reshape(1, 16), own, other, back_y, t["expand_x"], t["inverse_z"])


def solution(mesh):
    return jax.shard_map(
        on_device,
        mesh=mesh,
        in_specs=(P(None, None, "px", "py", None), P("px", "py", None, None, None, None), P(), P()),
        out_specs=P(None, None, "px", "py", None),
        check_vma=False,
    )
```

```python
import math

import jax
import jax.numpy as jnp
import numpy as np
from jax import lax
from jax.experimental import pallas as pl
from jax.experimental.pallas import tpu as pltpu
from jax.sharding import PartitionSpec as P

GRID = 256
CHANNELS = 16
MODES = 16
SLICES = 2
BLOCK = 16
RANK = 8
EVEN = RANK // 2
HALF = RANK * MODES
LANES = 2 * HALF
Z_CHIPS = 8
GROUP = 4
GROUPS = BLOCK // GROUP
ROWS = 128
VMEM = 24 * 1024 * 1024
CENTRE = (BLOCK - 1) / 2


def make_tables():
    freq = np.concatenate([np.arange(8), np.arange(-8, 0)]).astype(np.float64)
    turn = 2.0 * np.pi / GRID
    u = np.arange(BLOCK) - CENTRE
    basis, weight = [], []
    for part in (np.cos(np.outer(u, turn * freq)), np.sin(np.outer(u, turn * freq))):
        left, scale, right = np.linalg.svd(part)
        basis.append(left[:, :EVEN])
        weight.append(scale[:EVEN, None] * right[:EVEN])
    basis = np.concatenate(basis, axis=1)
    weight = np.concatenate(weight, axis=0)
    odd = np.arange(RANK) >= EVEN

    kz, z = np.arange(MODES), np.arange(GRID)
    angle = turn * np.outer(z, kz)
    depth = np.stack([np.cos(angle), -np.sin(angle)], axis=1)
    forward_z = np.repeat(depth[:, :, None, :], RANK, axis=2).reshape(GRID, LANES)
    w = np.where(kz == 0, 1.0, 2.0) * (0.5 / math.sqrt(MODES**3))
    inverse_z = (depth * w).transpose(1, 2, 0).reshape(2 * MODES, GRID)
    expand_x = np.einsum("xr,ab->arxb", basis, np.eye(2)).reshape(16, 32)
    expand_x = np.repeat(expand_x, MODES, axis=1)
    lanes_x = np.tile(np.repeat(basis, MODES, axis=1), (1, 2))

    forward_y = np.zeros((16, 16, 2, 16, 16))
    inverse_y = np.zeros((16, 16, 2, 16, 16))
    scale = float(GRID) ** -1.5
    for q in range(16):
        for s in range(2):
            for chip in range(Z_CHIPS):
                theta = turn * freq[2 * chip + ((q % 2) ^ s)] * (16 * q + np.arange(16))
                row = s * Z_CHIPS + chip
                forward_y[q, row, 0] = (np.cos(theta) * scale)[None, :]
                forward_y[q, row, 1] = (np.sin(theta) * scale)[None, :]
                inverse_y[q, :, 0, row] = np.cos(theta)[:, None]
                inverse_y[q, :, 1, row] = -np.sin(theta)[:, None]

    phase = turn * np.outer(freq, 16 * np.arange(16) + CENTRE)
    forward_x = np.stack([np.cos(phase), np.sin(phase)], axis=1)
    forward_x = np.repeat(forward_x[..., None], CHANNELS, axis=3).reshape(16, 512)
    lanes_v = np.tile(np.repeat(weight.T, MODES, axis=1), (1, 2))
    inverse_x = np.zeros((16, 2, RANK, 2, MODES))
    for p in range(16):
        cos, sin = np.cos(phase[:, p]) * weight, np.sin(phase[:, p]) * weight
        real, imag = np.stack([cos, -sin], axis=1), np.stack([sin, cos], axis=1)
        turned = odd[:, None, None]
        inverse_x[p, 0] = np.where(turned, -imag, real)
        inverse_x[p, 1] = np.where(turned, real, imag)
    inverse_x = inverse_x.reshape(16, 16, 32)

    tables = dict(
        forward_z=forward_z,
        inverse_z=inverse_z,
        expand_x=expand_x,
        lanes_x=lanes_x,
        forward_y=forward_y.reshape(16, 16, 512),
        inverse_y=inverse_y.reshape(16, 16, 512),
        forward_x=forward_x,
        lanes_v=lanes_v,
        inverse_x=inverse_x,
    )
    return {name: table.astype(np.float32) for name, table in tables.items()}


def iota(shape, dim):
    return lax.broadcasted_iota(jnp.int32, shape, dim)


def dot(a, b):
    return jnp.dot(a, b, preferred_element_type=jnp.float32)


def repeat_rows(table):
    rows, lanes = table.shape
    return jnp.broadcast_to(table[:, None, :], (rows, 16, lanes)).reshape(rows * 16, lanes)


def tile_rows(table):
    rows, lanes = table.shape
    return jnp.broadcast_to(table[None], (16, rows, lanes)).reshape(rows * 16, lanes)


def masked(table, keep):
    return jnp.where(keep, table, 0.0).astype(jnp.bfloat16)


def with_turned(data):
    turned = jnp.concatenate([data[:, HALF:], -data[:, :HALF]], axis=1)
    return jnp.concatenate([data, turned], axis=0).astype(jnp.bfloat16)


def own_frequencies(table):
    shape = (Z_CHIPS * 16, 512)
    return masked(repeat_rows(table), iota(shape, 0) % 16 == iota(shape, 1) % 256 // 16)


def forward_kernel(
    index_ref, field_hbm, table_z_hbm, lanes_x_hbm, table_y_hbm, back_y_hbm, back_x_hbm,
    sums_ref, send_ref, table_y_ref, back_y_ref, back_x_ref, first_ref, second_ref,
    rest, table_z_ref, lanes_x_ref, total, arrived, loaded,
):
    small = [
        pltpu.make_async_copy(source, target, loaded.at[i])
        for i, (source, target) in enumerate(
            [
                (table_y_hbm.at[index_ref[1]], table_y_ref),
                (table_z_hbm, table_z_ref),
                (lanes_x_hbm, lanes_x_ref),
                (back_y_hbm.at[index_ref[1]], back_y_ref),
                (back_x_hbm.at[index_ref[0]], back_x_ref),
            ]
        )
    ]
    for copy in small:
        copy.start()
    held = [first_ref, second_ref, rest.at[0], rest.at[1]]

    def fetch(g):
        return pltpu.make_async_copy(field_hbm.at[:, :, pl.ds(g * GROUP, GROUP)], held[g], arrived.at[g])

    for g in range(GROUPS):
        fetch(g).start()

    small[0].wait()
    table_y = own_frequencies(table_y_ref[Z_CHIPS:, :])
    for copy in small[1:]:
        copy.wait()

    table = jnp.concatenate(
        [(table_z_ref[...] * lanes_x_ref[x : x + 1, :]).astype(jnp.bfloat16) for x in range(BLOCK)], axis=0
    )
    for g in range(GROUPS):
        fetch(g).wait()
    data = jnp.concatenate(
        [held[g][:, :, j].reshape(SLICES * 256, GRID) for g in range(GROUPS) for j in range(GROUP)], axis=1
    )
    total[...] = dot(data, table)

    for b in range(SLICES):
        sums = total[b * 256 : (b + 1) * 256, :]
        sums_ref[b] = sums.astype(jnp.bfloat16)
        send = dot(table_y, with_turned(sums))
        send_ref[:, b] = send.reshape(Z_CHIPS, CHANNELS, LANES).astype(jnp.bfloat16)


def keep_kernel(sums_ref, table_y_ref, weight_ref, keep_ref, packed_ref):
    table_y = own_frequencies(table_y_ref[:Z_CHIPS, :])
    for b in range(SLICES):
        keep_ref[:, b] = dot(table_y, with_turned(sums_ref[b].astype(jnp.float32))).reshape(Z_CHIPS, CHANNELS, LANES)

    place = (iota((MODES, LANES), 0) == iota((MODES, LANES), 1) % MODES).astype(jnp.bfloat16)
    rows = iota((512, LANES), 0) % 16
    gather = (iota((32, 512), 0) == iota((32, 512), 1) // 16).astype(jnp.bfloat16)
    wide = dot(weight_ref[...].astype(jnp.bfloat16), place)
    wide = masked(wide, rows == iota((512, LANES), 1) // MODES)
    packed_ref[...] = dot(gather, wide).astype(jnp.bfloat16)


def sum_kernel(parts_ref, packed_ref, out_ref):
    parts = parts_ref[...].astype(jnp.float32)
    sums = jnp.sum(parts, axis=0).reshape(32, LANES).astype(jnp.bfloat16)
    message = jnp.concatenate([sums, packed_ref[...]], axis=0)
    out_ref[...] = jnp.broadcast_to(message[None], out_ref.shape)


def mix_kernel(got_ref, table_x_ref, lanes_v_ref, back_x_ref, out_ref):
    shape = (LANES, LANES)
    row, lane = iota(shape, 0), iota(shape, 1)
    kind = jnp.where(row % HALF // MODES < EVEN, 0, 1)
    step = jnp.where(row < HALF, 0, 1) - jnp.where(lane < HALF, 0, 1)
    fold = jnp.where(kind == 0, jnp.where(step == 0, 1.0, 0.0), step.astype(jnp.float32))
    fold = masked(fold, row % MODES == lane % MODES)
    shape = (RANK * 128, 128)
    row, lane = iota(shape, 0), iota(shape, 1)
    spread = masked(jnp.where(row // 128 == lane // MODES, 1.0, 0.0), row % MODES == lane % MODES)

    shape = (256, 512)
    table_x = masked(repeat_rows(table_x_ref[...]), iota(shape, 0) % 16 == iota(shape, 1) % 16)
    scale = repeat_rows(lanes_v_ref[...])
    mixed = []
    for b in range(SLICES):
        data = got_ref[:, b * 16 : (b + 1) * 16, :].reshape(256, LANES).astype(jnp.float32)
        modes = dot(table_x, with_turned(data)) * scale
        modes = dot(modes.astype(jnp.bfloat16), fold).reshape(MODES, CHANNELS, LANES)
        real, imag = modes[..., :HALF], modes[..., HALF:]
        for h in range(2):
            lanes = slice(h * HALF, (h + 1) * HALF)
            w_real = got_ref[:, 32:48, lanes].astype(jnp.float32)
            w_imag = got_ref[:, 48:64, lanes].astype(jnp.float32)
            out_real = jnp.sum(real * w_real - imag * w_imag, axis=1)
            out_imag = jnp.sum(real * w_imag + imag * w_real, axis=1)
            mixed.append(jnp.concatenate([out_real, out_imag], axis=0))
    mixed = jnp.concatenate(mixed, axis=1)
    mixed = mixed.astype(jnp.bfloat16).astype(jnp.float32)
    back = jnp.dot(
        back_x_ref[...], mixed, precision=lax.Precision.HIGHEST, preferred_element_type=jnp.float32
    )
    own = iota((8, 128), 0) == iota((8, 128), 1) // MODES
    rows = []
    for b in range(SLICES):
        for h in range(2):
            at = (2 * b + h) * 128
            for a in range(2):
                pieces = [
                    jnp.where(own, back[a * RANK + r : a * RANK + r + 1, at : at + 128], 0.0)
                    for r in range(RANK)
                ]
                rows.append(jnp.concatenate(pieces, axis=1))
    rows = jnp.concatenate(rows, axis=0).astype(jnp.bfloat16)
    rows = dot(rows, spread).reshape(SLICES, 2, 2, 8, HALF)
    for b in range(SLICES):
        half = [jnp.concatenate([rows[b, 0, a], rows[b, 1, a]], axis=0) for a in range(2)]
        message = jnp.concatenate(half, axis=1).astype(jnp.bfloat16)
        out_ref[:, b] = jnp.broadcast_to(message[None], (Z_CHIPS, CHANNELS, LANES))


def inverse_kernel(
    field_hbm, first_ref, second_ref, skip_ref, bias_ref, own_ref, other_ref,
    table_y_ref, expand_ref, table_z_ref,
    out_ref, rest, ready, arrived, sent,
):
    held = [first_ref, second_ref, rest.at[0], rest.at[1]]

    def fetch(g):
        return pltpu.make_async_copy(field_hbm.at[:, :, pl.ds(g * GROUP, GROUP)], held[g], arrived.at[g - 2])

    def store(g, j, count):
        return pltpu.make_async_copy(
            ready.at[g, :, :, pl.ds(j, count)],
            out_ref.at[:, :, pl.ds(g * GROUP + j, count)],
            sent.at[g + j],
        )

    for g in (2, 3):
        fetch(g).start()

    shape = (256, 256)
    place = (iota((16, 256), 0) == iota((16, 256), 1) // 16).astype(jnp.bfloat16)
    skip = repeat_rows(dot(skip_ref[...], place))
    skip = masked(skip, iota(shape, 0) % 16 == iota(shape, 1) % 16)
    one = iota((256, 16), 0) // 16 == iota((256, 16), 1)
    bias = jnp.sum(jnp.where(one, bias_ref[...], 0.0), axis=1, keepdims=True)
    parts = []
    for _ in range(3):
        parts.append(bias.astype(jnp.bfloat16).astype(jnp.float32))
        bias = bias - parts[-1]

    shape = (2 * MODES, GRID)
    ones = jnp.where(iota(shape, 0) == MODES, 1.0, 0.0)
    tables_z = []
    for j in range(GROUP):
        blocks = [ones, ones, ones, jnp.zeros(shape, jnp.float32)]
        blocks[j] = blocks[j] + table_z_ref[...]
        tables_z.append(jnp.concatenate(blocks, axis=0).astype(jnp.bfloat16))

    shape = (256, 512)
    table_y = masked(tile_rows(table_y_ref[...]), iota(shape, 0) // 16 == iota(shape, 1) % 16)
    expand = masked(repeat_rows(expand_ref[...]), iota(shape, 0) % 16 == iota(shape, 1) % 16)
    lane = iota(shape, 1) % 128
    modes = []
    for b in range(SLICES):
        data = [ref[:, b].reshape(128, LANES) for ref in (own_ref, other_ref)]
        data = jnp.concatenate(data, axis=0).astype(jnp.float32)
        rows = dot(table_y, with_turned(data)).astype(jnp.bfloat16)
        rows = dot(rows, expand)
        for j in range(3):
            rows = jnp.where(lane == 32 * j + 16, parts[j], rows)
        modes.append(rows.astype(jnp.bfloat16))

    stores = []
    for g in range(GROUPS):
        if g >= 2:
            fetch(g).wait()
        for j in range(GROUP):
            for b in range(SLICES):
                lhs = modes[b][:, g * 128 : (g + 1) * 128]
                for r in range(0, 256, ROWS):
                    value = dot(lhs[r : r + ROWS], tables_z[j])
                    value = value + dot(skip[r : r + ROWS], held[g][b, :, j].reshape(256, GRID))
                    half = 0.5 * value
                    value = half + half * lax.erf(value * math.sqrt(0.5))
                    value = value.astype(jnp.bfloat16).reshape(ROWS // BLOCK, BLOCK, GRID)
                    ready[g, b, r // BLOCK : (r + ROWS) // BLOCK, j] = value
            if g == GROUPS - 1:
                stores.append(store(g, j, 1))
            elif j == GROUP - 1:
                stores.append(store(g, 0, GROUP))
            else:
                continue
            stores[-1].start()
    for copy in stores:
        copy.wait()


VM = pl.BlockSpec(memory_space=pltpu.VMEM)
SM = pl.BlockSpec(memory_space=pltpu.SMEM)
ANY = pl.BlockSpec(memory_space=pl.ANY)
PARAMS = pltpu.CompilerParams(vmem_limit_bytes=VMEM)
PAIR = [(i, i ^ 1) for i in range(16)]
CHIPS = [list(range(0, 16, 2)), list(range(1, 16, 2))]


def shape_of(shape, dtype):
    return jax.ShapeDtypeStruct(shape, dtype)


def on_device(field, spectral_weight, skip_weight, bias):
    t = make_tables()
    f32, bf16 = jnp.float32, jnp.bfloat16
    place = jnp.stack([lax.axis_index("px"), lax.axis_index("py")]).astype(jnp.int32)
    planes = (SLICES, CHANNELS, GROUP, BLOCK, GRID)
    part = (Z_CHIPS, SLICES, CHANNELS, LANES)

    far = [
        pltpu.with_memory_space_constraint(a, pltpu.HBM)
        for a in (
            field, t["forward_z"], t["lanes_x"], t["forward_y"],
            t["inverse_y"], t["inverse_x"],
        )
    ]
    sums, send, table_y, back_y, back_x, *held = pl.pallas_call(
        forward_kernel,
        name="forward",
        in_specs=[SM] + [ANY] * 6,
        out_specs=[VM] * 7,
        out_shape=[
            shape_of((SLICES, 256, LANES), bf16),
            shape_of(part, bf16),
            shape_of((16, 512), f32),
            shape_of((16, 512), f32),
            shape_of((16, 32), f32),
            pltpu.VMEM(planes, bf16),
            pltpu.VMEM(planes, bf16),
        ],
        scratch_shapes=[
            pltpu.VMEM((2, *planes), bf16),
            pltpu.VMEM((GRID, LANES), f32),
            pltpu.VMEM((BLOCK, LANES), f32),
            pltpu.VMEM((512, LANES), f32),
            pltpu.SemaphoreType.DMA((GROUPS,)),
            pltpu.SemaphoreType.DMA((5,)),
        ],
        compiler_params=PARAMS,
    )(place, *far)
    got = lax.ppermute(send, "py", PAIR)
    keep, packed = pl.pallas_call(
        keep_kernel,
        name="keep",
        in_specs=[VM, VM, VM],
        out_specs=[VM, VM],
        out_shape=[shape_of(part, f32), shape_of((32, LANES), bf16)],
        compiler_params=PARAMS,
        cost_estimate=pl.CostEstimate(flops=2 * 2 * 128 * 512 * 256, bytes_accessed=1 << 20, transcendentals=0),
    )(sums, table_y, spectral_weight.reshape(512, MODES))
    sums = (keep + got.astype(f32)).astype(bf16)
    sums = lax.all_to_all(sums, "py", 0, 0, axis_index_groups=CHIPS, tiled=True)
    message = pl.pallas_call(
        sum_kernel,
        name="sum",
        in_specs=[VM, VM],
        out_specs=VM,
        out_shape=shape_of((16, 64, LANES), bf16),
        compiler_params=PARAMS,
    )(sums, packed)
    message = lax.all_to_all(message, "px", 0, 0, tiled=True)
    message = pl.pallas_call(
        mix_kernel,
        name="mix",
        in_specs=[VM, VM, VM, VM],
        out_specs=VM,
        out_shape=shape_of(part, bf16),
        compiler_params=PARAMS,
    )(message, t["forward_x"], t["lanes_v"], back_x)
    own = lax.all_to_all(message, "py", 0, 0, axis_index_groups=CHIPS, tiled=True)
    other = lax.ppermute(own, "py", PAIR)
    return pl.pallas_call(
        inverse_kernel,
        name="inverse",
        in_specs=[ANY] + [VM] * 9,
        out_specs=ANY,
        out_shape=shape_of(field.shape, bf16),
        scratch_shapes=[
            pltpu.VMEM((2, *planes), bf16),
            pltpu.VMEM((GROUPS, *planes), bf16),
            pltpu.SemaphoreType.DMA((2,)),
            pltpu.SemaphoreType.DMA((GROUPS + GROUP - 1,)),
        ],
        compiler_params=PARAMS,
    )(far[0], *held, skip_weight, bias.reshape(1, 16), own, other, back_y, t["expand_x"], t["inverse_z"])


def solution(mesh):
    return jax.shard_map(
        on_device,
        mesh=mesh,
        in_specs=(P(None, None, "px", "py", None), P("px", "py", None, None, None, None), P(), P()),
        out_specs=P(None, None, "px", "py", None),
        check_vma=False,
    )
```

```python
import math

import jax
import jax.numpy as jnp
import numpy as np
from jax import lax
from jax.experimental import pallas as pl
from jax.experimental.pallas import tpu as pltpu
from jax.sharding import PartitionSpec as P

GRID = 256
CHANNELS = 16
MODES = 16
SLICES = 2
BLOCK = 16
RANK = 8
EVEN = RANK // 2
HALF = RANK * MODES
LANES = 2 * HALF
Z_CHIPS = 8
GROUP = 4
GROUPS = BLOCK // GROUP
ROWS = 128
VMEM = 24 * 1024 * 1024
CENTRE = (BLOCK - 1) / 2


def make_tables():
    freq = np.concatenate([np.arange(8), np.arange(-8, 0)]).astype(np.float64)
    turn = 2.0 * np.pi / GRID
    u = np.arange(BLOCK) - CENTRE
    basis, weight = [], []
    for part in (np.cos(np.outer(u, turn * freq)), np.sin(np.outer(u, turn * freq))):
        left, scale, right = np.linalg.svd(part)
        basis.append(left[:, :EVEN])
        weight.append(scale[:EVEN, None] * right[:EVEN])
    basis = np.concatenate(basis, axis=1)
    weight = np.concatenate(weight, axis=0)
    odd = np.arange(RANK) >= EVEN

    kz, z = np.arange(MODES), np.arange(GRID)
    angle = turn * np.outer(z, kz)
    depth = np.stack([np.cos(angle), -np.sin(angle)], axis=1)
    forward_z = np.repeat(depth[:, :, None, :], RANK, axis=2).reshape(GRID, LANES)
    w = np.where(kz == 0, 1.0, 2.0) * (0.5 / math.sqrt(MODES**3))
    inverse_z = (depth * w).transpose(1, 2, 0).reshape(2 * MODES, GRID)
    expand_x = np.einsum("xr,ab->arxb", basis, np.eye(2)).reshape(16, 32)
    expand_x = np.repeat(expand_x, MODES, axis=1)
    lanes_x = np.tile(np.repeat(basis, MODES, axis=1), (1, 2))

    forward_y = np.zeros((16, 16, 2, 16, 16))
    inverse_y = np.zeros((16, 16, 2, 16, 16))
    scale = float(GRID) ** -1.5
    for q in range(16):
        for s in range(2):
            for chip in range(Z_CHIPS):
                theta = turn * freq[2 * chip + ((q % 2) ^ s)] * (16 * q + np.arange(16))
                row = s * Z_CHIPS + chip
                forward_y[q, row, 0] = (np.cos(theta) * scale)[None, :]
                forward_y[q, row, 1] = (np.sin(theta) * scale)[None, :]
                inverse_y[q, :, 0, row] = np.cos(theta)[:, None]
                inverse_y[q, :, 1, row] = -np.sin(theta)[:, None]

    phase = turn * np.outer(freq, 16 * np.arange(16) + CENTRE)
    forward_x = np.stack([np.cos(phase), np.sin(phase)], axis=1)
    forward_x = np.repeat(forward_x[..., None], CHANNELS, axis=3).reshape(16, 512)
    lanes_v = np.tile(np.repeat(weight.T, MODES, axis=1), (1, 2))
    inverse_x = np.zeros((16, 2, RANK, 2, MODES))
    for p in range(16):
        cos, sin = np.cos(phase[:, p]) * weight, np.sin(phase[:, p]) * weight
        real, imag = np.stack([cos, -sin], axis=1), np.stack([sin, cos], axis=1)
        turned = odd[:, None, None]
        inverse_x[p, 0] = np.where(turned, -imag, real)
        inverse_x[p, 1] = np.where(turned, real, imag)
    inverse_x = inverse_x.reshape(16, 16, 32)

    tables = dict(
        forward_z=forward_z,
        inverse_z=inverse_z,
        expand_x=expand_x,
        lanes_x=lanes_x,
        forward_y=forward_y.reshape(16, 16, 512),
        inverse_y=inverse_y.reshape(16, 16, 512),
        forward_x=forward_x,
        lanes_v=lanes_v,
        inverse_x=inverse_x,
    )
    return {name: table.astype(np.float32) for name, table in tables.items()}


def iota(shape, dim):
    return lax.broadcasted_iota(jnp.int32, shape, dim)


def dot(a, b):
    return jnp.dot(a, b, preferred_element_type=jnp.float32)


def repeat_rows(table):
    rows, lanes = table.shape
    return jnp.broadcast_to(table[:, None, :], (rows, 16, lanes)).reshape(rows * 16, lanes)


def tile_rows(table):
    rows, lanes = table.shape
    return jnp.broadcast_to(table[None], (16, rows, lanes)).reshape(rows * 16, lanes)


def masked(table, keep):
    return jnp.where(keep, table, 0.0).astype(jnp.bfloat16)


def with_turned(data):
    turned = jnp.concatenate([data[:, HALF:], -data[:, :HALF]], axis=1)
    return jnp.concatenate([data, turned], axis=0).astype(jnp.bfloat16)


def own_frequencies(table):
    shape = (Z_CHIPS * 16, 512)
    return masked(repeat_rows(table), iota(shape, 0) % 16 == iota(shape, 1) % 256 // 16)


def forward_kernel(
    index_ref, field_hbm, table_z_hbm, lanes_x_hbm, table_y_hbm, back_y_hbm, back_x_hbm,
    sums_ref, send_ref, table_y_ref, back_y_ref, back_x_ref, held0, held1, held2, held3,
    table_z_ref, lanes_x_ref, total, arrived, loaded,
):
    small = [
        pltpu.make_async_copy(source, target, loaded.at[i])
        for i, (source, target) in enumerate(
            [
                (table_y_hbm.at[index_ref[1]], table_y_ref),
                (table_z_hbm, table_z_ref),
                (lanes_x_hbm, lanes_x_ref),
                (back_y_hbm.at[index_ref[1]], back_y_ref),
                (back_x_hbm.at[index_ref[0]], back_x_ref),
            ]
        )
    ]
    for copy in small:
        copy.start()
    held = [held0, held1, held2, held3]

    def fetch(g):
        return pltpu.make_async_copy(field_hbm.at[:, :, pl.ds(g * GROUP, GROUP)], held[g], arrived.at[g])

    for g in range(GROUPS):
        fetch(g).start()

    small[0].wait()
    table_y = own_frequencies(table_y_ref[Z_CHIPS:, :])
    for copy in small[1:]:
        copy.wait()

    table = jnp.concatenate(
        [(table_z_ref[...] * lanes_x_ref[x : x + 1, :]).astype(jnp.bfloat16) for x in range(BLOCK)], axis=0
    )
    for g in range(GROUPS):
        fetch(g).wait()
    data = jnp.concatenate(
        [held[g][:, :, j].reshape(SLICES * 256, GRID) for g in range(GROUPS) for j in range(GROUP)], axis=1
    )
    total[...] = dot(data, table)

    for b in range(SLICES):
        sums = total[b * 256 : (b + 1) * 256, :]
        sums_ref[b] = sums.astype(jnp.bfloat16)
        send = dot(table_y, with_turned(sums))
        send_ref[:, b] = send.reshape(Z_CHIPS, CHANNELS, LANES).astype(jnp.bfloat16)


def keep_kernel(sums_ref, table_y_ref, weight_ref, keep_ref, packed_ref):
    table_y = own_frequencies(table_y_ref[:Z_CHIPS, :])
    for b in range(SLICES):
        keep_ref[:, b] = dot(table_y, with_turned(sums_ref[b].astype(jnp.float32))).reshape(Z_CHIPS, CHANNELS, LANES)

    place = (iota((MODES, LANES), 0) == iota((MODES, LANES), 1) % MODES).astype(jnp.bfloat16)
    rows = iota((512, LANES), 0) % 16
    gather = (iota((32, 512), 0) == iota((32, 512), 1) // 16).astype(jnp.bfloat16)
    wide = dot(weight_ref[...].astype(jnp.bfloat16), place)
    wide = masked(wide, rows == iota((512, LANES), 1) // MODES)
    packed_ref[...] = dot(gather, wide).astype(jnp.bfloat16)


def sum_kernel(parts_ref, packed_ref, out_ref):
    parts = parts_ref[...].astype(jnp.float32)
    sums = jnp.sum(parts, axis=0).reshape(32, LANES).astype(jnp.bfloat16)
    message = jnp.concatenate([sums, packed_ref[...]], axis=0)
    out_ref[...] = jnp.broadcast_to(message[None], out_ref.shape)


def mix_kernel(got_ref, table_x_ref, lanes_v_ref, back_x_ref, out_ref):
    shape = (LANES, LANES)
    row, lane = iota(shape, 0), iota(shape, 1)
    kind = jnp.where(row % HALF // MODES < EVEN, 0, 1)
    step = jnp.where(row < HALF, 0, 1) - jnp.where(lane < HALF, 0, 1)
    fold = jnp.where(kind == 0, jnp.where(step == 0, 1.0, 0.0), step.astype(jnp.float32))
    fold = masked(fold, row % MODES == lane % MODES)
    shape = (RANK * 128, 128)
    row, lane = iota(shape, 0), iota(shape, 1)
    spread = masked(jnp.where(row // 128 == lane // MODES, 1.0, 0.0), row % MODES == lane % MODES)

    shape = (256, 512)
    table_x = masked(repeat_rows(table_x_ref[...]), iota(shape, 0) % 16 == iota(shape, 1) % 16)
    scale = repeat_rows(lanes_v_ref[...])
    mixed = []
    for b in range(SLICES):
        data = got_ref[:, b * 16 : (b + 1) * 16, :].reshape(256, LANES).astype(jnp.float32)
        modes = dot(table_x, with_turned(data)) * scale
        modes = dot(modes.astype(jnp.bfloat16), fold).reshape(MODES, CHANNELS, LANES)
        real, imag = modes[..., :HALF], modes[..., HALF:]
        for h in range(2):
            lanes = slice(h * HALF, (h + 1) * HALF)
            w_real = got_ref[:, 32:48, lanes].astype(jnp.float32)
            w_imag = got_ref[:, 48:64, lanes].astype(jnp.float32)
            out_real = jnp.sum(real * w_real - imag * w_imag, axis=1)
            out_imag = jnp.sum(real * w_imag + imag * w_real, axis=1)
            mixed.append(jnp.concatenate([out_real, out_imag], axis=0))
    mixed = jnp.concatenate(mixed, axis=1)
    mixed = mixed.astype(jnp.bfloat16).astype(jnp.float32)
    back = jnp.dot(
        back_x_ref[...], mixed, precision=lax.Precision.HIGHEST, preferred_element_type=jnp.float32
    )
    own = iota((8, 128), 0) == iota((8, 128), 1) // MODES
    rows = []
    for b in range(SLICES):
        for h in range(2):
            at = (2 * b + h) * 128
            for a in range(2):
                pieces = [
                    jnp.where(own, back[a * RANK + r : a * RANK + r + 1, at : at + 128], 0.0)
                    for r in range(RANK)
                ]
                rows.append(jnp.concatenate(pieces, axis=1))
    rows = jnp.concatenate(rows, axis=0).astype(jnp.bfloat16)
    rows = dot(rows, spread).reshape(SLICES, 2, 2, 8, HALF)
    for b in range(SLICES):
        half = [jnp.concatenate([rows[b, 0, a], rows[b, 1, a]], axis=0) for a in range(2)]
        message = jnp.concatenate(half, axis=1).astype(jnp.bfloat16)
        out_ref[:, b] = jnp.broadcast_to(message[None], (Z_CHIPS, CHANNELS, LANES))


def prepare_kernel(
    skip_ref, bias_ref, own_ref, table_y_ref, basis_ref, table_z_ref,
    left_ref, parts_ref, rows_z_ref, expand_ref, other_y_ref, modes_ref,
):
    shape = (256, 256)
    place = (iota((16, 256), 0) == iota((16, 256), 1) // 16).astype(jnp.bfloat16)
    skip = repeat_rows(dot(skip_ref[...], place))
    left_ref[...] = masked(skip, iota(shape, 0) % 16 == iota(shape, 1) % 16)
    one = iota((256, 16), 0) // 16 == iota((256, 16), 1)
    bias = jnp.sum(jnp.where(one, bias_ref[...], 0.0), axis=1, keepdims=True)
    for j in range(3):
        part = bias.astype(jnp.bfloat16).astype(jnp.float32)
        parts_ref[j] = jnp.broadcast_to(part, (256, 128))
        bias = bias - part

    shape = (2 * MODES, GRID)
    ones = jnp.where(iota(shape, 0) == MODES, 1.0, 0.0)
    for j in range(GROUP):
        blocks = [ones, ones, ones, jnp.zeros(shape, jnp.float32)]
        blocks[j] = blocks[j] + table_z_ref[...]
        rows_z_ref[j] = jnp.concatenate(blocks, axis=0).astype(jnp.bfloat16)

    shape = (256, 512)
    table = masked(tile_rows(table_y_ref[...]), iota(shape, 0) // 16 == iota(shape, 1) % 16)
    expand_ref[...] = masked(repeat_rows(basis_ref[...]), iota(shape, 0) % 16 == iota(shape, 1) % 16)
    own = jnp.concatenate([table[:, 0:128], table[:, 256:384]], axis=1)
    other_y_ref[...] = jnp.concatenate([table[:, 128:256], table[:, 384:512]], axis=1)
    for b in range(SLICES):
        data = own_ref[:, b].reshape(128, LANES).astype(jnp.float32)
        modes_ref[b] = dot(own, with_turned(data))


def inverse_kernel(
    held0, held1, held2, held3, left_ref, parts_ref, table_z_ref, expand_ref, table_y_ref, modes_ref, other_ref,
    out_ref, ready, sent,
):
    held = [held0, held1, held2, held3]

    def store(g, j, count):
        return pltpu.make_async_copy(
            ready.at[g, :, :, pl.ds(j, count)],
            out_ref.at[:, :, pl.ds(g * GROUP + j, count)],
            sent.at[g + j],
        )

    skip = left_ref[...]
    tables_z = [table_z_ref[j] for j in range(GROUP)]
    lane = iota((256, 512), 1) % 128
    modes = []
    for b in range(SLICES):
        data = other_ref[:, b].reshape(128, LANES).astype(jnp.float32)
        rows = modes_ref[b] + dot(table_y_ref[...], with_turned(data))
        rows = dot(rows.astype(jnp.bfloat16), expand_ref[...])
        for j in range(3):
            part = jnp.concatenate([parts_ref[j]] * 4, axis=1)
            rows = jnp.where(lane == 32 * j + 16, part, rows)
        modes.append(rows.astype(jnp.bfloat16))

    stores = []
    for g in range(GROUPS):
        for j in range(GROUP):
            for b in range(SLICES):
                lhs = modes[b][:, g * 128 : (g + 1) * 128]
                for r in range(0, 256, ROWS):
                    value = dot(lhs[r : r + ROWS], tables_z[j])
                    value = value + dot(skip[r : r + ROWS], held[g][b, :, j].reshape(256, GRID))
                    half = 0.5 * value
                    value = half + half * lax.erf(value * math.sqrt(0.5))
                    value = value.astype(jnp.bfloat16).reshape(ROWS // BLOCK, BLOCK, GRID)
                    ready[g, b, r // BLOCK : (r + ROWS) // BLOCK, j] = value
            if g == GROUPS - 1:
                stores.append(store(g, j, 1))
            elif j == GROUP - 1:
                stores.append(store(g, 0, GROUP))
            else:
                continue
            stores[-1].start()
    for copy in stores:
        copy.wait()


VM = pl.BlockSpec(memory_space=pltpu.VMEM)
SM = pl.BlockSpec(memory_space=pltpu.SMEM)
ANY = pl.BlockSpec(memory_space=pl.ANY)
PARAMS = pltpu.CompilerParams(vmem_limit_bytes=VMEM)
PAIR = [(i, i ^ 1) for i in range(16)]
CHIPS = [list(range(0, 16, 2)), list(range(1, 16, 2))]


def shape_of(shape, dtype):
    return jax.ShapeDtypeStruct(shape, dtype)


def on_device(field, spectral_weight, skip_weight, bias):
    t = make_tables()
    f32, bf16 = jnp.float32, jnp.bfloat16
    place = jnp.stack([lax.axis_index("px"), lax.axis_index("py")]).astype(jnp.int32)
    planes = (SLICES, CHANNELS, GROUP, BLOCK, GRID)
    part = (Z_CHIPS, SLICES, CHANNELS, LANES)

    far = [
        pltpu.with_memory_space_constraint(a, pltpu.HBM)
        for a in (
            field, t["forward_z"], t["lanes_x"], t["forward_y"],
            t["inverse_y"], t["inverse_x"],
        )
    ]
    sums, send, table_y, back_y, back_x, *held = pl.pallas_call(
        forward_kernel,
        name="forward",
        in_specs=[SM] + [ANY] * 6,
        out_specs=[VM] * (5 + GROUPS),
        out_shape=[
            shape_of((SLICES, 256, LANES), bf16),
            shape_of(part, bf16),
            shape_of((16, 512), f32),
            shape_of((16, 512), f32),
            shape_of((16, 32), f32),
            *[pltpu.VMEM(planes, bf16)] * GROUPS,
        ],
        scratch_shapes=[
            pltpu.VMEM((GRID, LANES), f32),
            pltpu.VMEM((BLOCK, LANES), f32),
            pltpu.VMEM((512, LANES), f32),
            pltpu.SemaphoreType.DMA((GROUPS,)),
            pltpu.SemaphoreType.DMA((5,)),
        ],
        compiler_params=PARAMS,
    )(place, *far)
    got = lax.ppermute(send, "py", PAIR)
    keep, packed = pl.pallas_call(
        keep_kernel,
        name="keep",
        in_specs=[VM, VM, VM],
        out_specs=[VM, VM],
        out_shape=[shape_of(part, f32), shape_of((32, LANES), bf16)],
        compiler_params=PARAMS,
        cost_estimate=pl.CostEstimate(flops=2 * 2 * 128 * 512 * 256, bytes_accessed=1 << 20, transcendentals=0),
    )(sums, table_y, spectral_weight.reshape(512, MODES))
    sums = (keep + got.astype(f32)).astype(bf16)
    sums = lax.all_to_all(sums, "py", 0, 0, axis_index_groups=CHIPS, tiled=True)
    message = pl.pallas_call(
        sum_kernel,
        name="sum",
        in_specs=[VM, VM],
        out_specs=VM,
        out_shape=shape_of((16, 64, LANES), bf16),
        compiler_params=PARAMS,
    )(sums, packed)
    message = lax.all_to_all(message, "px", 0, 0, tiled=True)
    message = pl.pallas_call(
        mix_kernel,
        name="mix",
        in_specs=[VM, VM, VM, VM],
        out_specs=VM,
        out_shape=shape_of(part, bf16),
        compiler_params=PARAMS,
    )(message, t["forward_x"], t["lanes_v"], back_x)
    own = lax.all_to_all(message, "py", 0, 0, axis_index_groups=CHIPS, tiled=True)
    other = lax.ppermute(own, "py", PAIR)
    prepared = pl.pallas_call(
        prepare_kernel,
        name="prepare",
        in_specs=[VM] * 6,
        out_specs=[VM] * 6,
        out_shape=[
            shape_of((256, 256), bf16),
            shape_of((3, 256, 128), f32),
            shape_of((GROUP, 128, GRID), bf16),
            shape_of((LANES, 512), bf16),
            shape_of((256, 256), bf16),
            shape_of((SLICES, 256, LANES), f32),
        ],
        compiler_params=PARAMS,
        cost_estimate=pl.CostEstimate(flops=2 * 2 * 256 * 256 * 256, bytes_accessed=1 << 20, transcendentals=0),
    )(skip_weight, bias.reshape(1, 16), own, back_y, t["expand_x"], t["inverse_z"])
    return pl.pallas_call(
        inverse_kernel,
        name="inverse",
        in_specs=[VM] * (7 + GROUPS),
        out_specs=ANY,
        out_shape=shape_of(field.shape, bf16),
        scratch_shapes=[
            pltpu.VMEM((GROUPS, *planes), bf16),
            pltpu.SemaphoreType.DMA((GROUPS + GROUP - 1,)),
        ],
        compiler_params=PARAMS,
    )(*held, *prepared, other)


def solution(mesh):
    return jax.shard_map(
        on_device,
        mesh=mesh,
        in_specs=(P(None, None, "px", "py", None), P("px", "py", None, None, None, None), P(), P()),
        out_specs=P(None, None, "px", "py", None),
        check_vma=False,
    )
```

```python
import math

import jax
import jax.numpy as jnp
import numpy as np
from jax import lax
from jax.experimental import pallas as pl
from jax.experimental.pallas import tpu as pltpu
from jax.sharding import PartitionSpec as P

GRID = 256
CHANNELS = 16
MODES = 16
SLICES = 2
BLOCK = 16
RANK = 8
EVEN = RANK // 2
HALF = RANK * MODES
LANES = 2 * HALF
Z_CHIPS = 8
GROUP = 4
GROUPS = BLOCK // GROUP
ROWS = 128
VMEM = 24 * 1024 * 1024
CENTRE = (BLOCK - 1) / 2
CHIP_ORDER = (4, 5, 6, 7, 0, 1, 2, 3)
BLOCK_ORDER = (10, 11, 8, 9, 14, 15, 12, 13, 2, 3, 0, 1, 6, 7, 4, 5)


def make_tables():
    freq = np.concatenate([np.arange(8), np.arange(-8, 0)]).astype(np.float64)
    turn = 2.0 * np.pi / GRID
    u = np.arange(BLOCK) - CENTRE
    basis, weight = [], []
    for part in (np.cos(np.outer(u, turn * freq)), np.sin(np.outer(u, turn * freq))):
        left, scale, right = np.linalg.svd(part)
        basis.append(left[:, :EVEN])
        weight.append(scale[:EVEN, None] * right[:EVEN])
    basis = np.concatenate(basis, axis=1)
    weight = np.concatenate(weight, axis=0)
    odd = np.arange(RANK) >= EVEN

    kz, z = np.arange(MODES), np.arange(GRID)
    angle = turn * np.outer(z, kz)
    depth = np.stack([np.cos(angle), -np.sin(angle)], axis=1)
    forward_z = np.repeat(depth[:, :, None, :], RANK, axis=2).reshape(GRID, LANES)
    w = np.where(kz == 0, 1.0, 2.0) * (0.5 / math.sqrt(MODES**3))
    inverse_z = (depth * w).transpose(1, 2, 0).reshape(2 * MODES, GRID)
    expand_x = np.einsum("xr,ab->arxb", basis, np.eye(2)).reshape(16, 32)
    expand_x = np.repeat(expand_x, MODES, axis=1)
    lanes_x = np.tile(np.repeat(basis, MODES, axis=1), (1, 2))

    forward_y = np.zeros((16, 16, 2, 16, 16))
    inverse_y = np.zeros((16, 16, 2, 16, 16))
    scale = float(GRID) ** -1.5
    for q in range(16):
        for s in range(2):
            for chip in range(Z_CHIPS):
                theta = turn * freq[2 * CHIP_ORDER[chip] + ((q % 2) ^ s)] * (16 * q + np.arange(16))
                row = s * Z_CHIPS + chip
                forward_y[q, row, 0] = (np.cos(theta) * scale)[None, :]
                forward_y[q, row, 1] = (np.sin(theta) * scale)[None, :]
                inverse_y[q, :, 0, row] = np.cos(theta)[:, None]
                inverse_y[q, :, 1, row] = -np.sin(theta)[:, None]

    order = list(BLOCK_ORDER)
    phase = turn * np.outer(freq[order], 16 * np.arange(16) + CENTRE)
    weight = weight[:, order]
    forward_x = np.stack([np.cos(phase), np.sin(phase)], axis=1)[..., order]
    forward_x = np.repeat(forward_x[..., None], CHANNELS, axis=3).reshape(16, 512)
    lanes_v = np.tile(np.repeat(weight.T, MODES, axis=1), (1, 2))
    inverse_x = np.zeros((16, 2, RANK, 2, MODES))
    for p in range(16):
        cos, sin = np.cos(phase[:, p]) * weight, np.sin(phase[:, p]) * weight
        real, imag = np.stack([cos, -sin], axis=1), np.stack([sin, cos], axis=1)
        turned = odd[:, None, None]
        inverse_x[p, 0] = np.where(turned, -imag, real)
        inverse_x[p, 1] = np.where(turned, real, imag)
    inverse_x = inverse_x.reshape(16, 16, 32)

    tables = dict(
        forward_z=forward_z,
        inverse_z=inverse_z,
        expand_x=expand_x,
        lanes_x=lanes_x,
        forward_y=forward_y.reshape(16, 16, 512),
        inverse_y=inverse_y.reshape(16, 16, 512),
        forward_x=forward_x,
        lanes_v=lanes_v,
        inverse_x=inverse_x,
    )
    return {name: table.astype(np.float32) for name, table in tables.items()}


def iota(shape, dim):
    return lax.broadcasted_iota(jnp.int32, shape, dim)


def dot(a, b):
    return jnp.dot(a, b, preferred_element_type=jnp.float32)


def repeat_rows(table):
    rows, lanes = table.shape
    return jnp.broadcast_to(table[:, None, :], (rows, 16, lanes)).reshape(rows * 16, lanes)


def tile_rows(table):
    rows, lanes = table.shape
    return jnp.broadcast_to(table[None], (16, rows, lanes)).reshape(rows * 16, lanes)


def masked(table, keep):
    return jnp.where(keep, table, 0.0).astype(jnp.bfloat16)


def with_turned(data):
    turned = jnp.concatenate([data[:, HALF:], -data[:, :HALF]], axis=1)
    return jnp.concatenate([data, turned], axis=0).astype(jnp.bfloat16)


def own_frequencies(table):
    shape = (Z_CHIPS * 16, 512)
    return masked(repeat_rows(table), iota(shape, 0) % 16 == iota(shape, 1) % 256 // 16)


def forward_kernel(
    index_ref, field_hbm, table_z_hbm, lanes_x_hbm, table_y_hbm, back_y_hbm, back_x_hbm,
    sums_ref, send_ref, table_y_ref, back_y_ref, back_x_ref, held0, held1, held2, held3,
    table_z_ref, lanes_x_ref, total, arrived, loaded,
):
    small = [
        pltpu.make_async_copy(source, target, loaded.at[i])
        for i, (source, target) in enumerate(
            [
                (table_y_hbm.at[index_ref[1]], table_y_ref),
                (table_z_hbm, table_z_ref),
                (lanes_x_hbm, lanes_x_ref),
                (back_y_hbm.at[index_ref[1]], back_y_ref),
                (back_x_hbm.at[index_ref[0]], back_x_ref),
            ]
        )
    ]
    for copy in small:
        copy.start()
    held = [held0, held1, held2, held3]

    def fetch(g):
        return pltpu.make_async_copy(field_hbm.at[:, :, pl.ds(g * GROUP, GROUP)], held[g], arrived.at[g])

    for g in range(GROUPS):
        fetch(g).start()

    small[0].wait()
    table_y = own_frequencies(table_y_ref[Z_CHIPS:, :])
    for copy in small[1:]:
        copy.wait()

    table = jnp.concatenate(
        [(table_z_ref[...] * lanes_x_ref[x : x + 1, :]).astype(jnp.bfloat16) for x in range(BLOCK)], axis=0
    )
    for g in range(GROUPS):
        fetch(g).wait()
    data = jnp.concatenate(
        [held[g][:, :, j].reshape(SLICES * 256, GRID) for g in range(GROUPS) for j in range(GROUP)], axis=1
    )
    total[...] = dot(data, table)

    for b in range(SLICES):
        sums = total[b * 256 : (b + 1) * 256, :]
        sums_ref[b] = sums.astype(jnp.bfloat16)
        send = dot(table_y, with_turned(sums))
        send_ref[:, b] = send.reshape(Z_CHIPS, CHANNELS, LANES).astype(jnp.bfloat16)


def keep_kernel(sums_ref, table_y_ref, weight_ref, keep_ref, packed_ref):
    table_y = own_frequencies(table_y_ref[:Z_CHIPS, :])
    for b in range(SLICES):
        keep_ref[:, b] = dot(table_y, with_turned(sums_ref[b].astype(jnp.float32))).reshape(Z_CHIPS, CHANNELS, LANES)

    place = (iota((MODES, LANES), 0) == iota((MODES, LANES), 1) % MODES).astype(jnp.bfloat16)
    rows = iota((512, LANES), 0) % 16
    gather = (iota((32, 512), 0) == iota((32, 512), 1) // 16).astype(jnp.bfloat16)
    wide = dot(weight_ref[...].astype(jnp.bfloat16), place)
    wide = masked(wide, rows == iota((512, LANES), 1) // MODES)
    packed_ref[...] = dot(gather, wide).astype(jnp.bfloat16)


def sum_kernel(parts_ref, packed_ref, out_ref):
    parts = parts_ref[...].astype(jnp.float32)
    sums = jnp.sum(parts, axis=0).reshape(32, LANES).astype(jnp.bfloat16)
    message = jnp.concatenate([sums, packed_ref[...]], axis=0)
    out_ref[...] = jnp.broadcast_to(message[None], out_ref.shape)


def mix_kernel(got_ref, table_x_ref, lanes_v_ref, back_x_ref, out_ref):
    shape = (LANES, LANES)
    row, lane = iota(shape, 0), iota(shape, 1)
    kind = jnp.where(row % HALF // MODES < EVEN, 0, 1)
    step = jnp.where(row < HALF, 0, 1) - jnp.where(lane < HALF, 0, 1)
    fold = jnp.where(kind == 0, jnp.where(step == 0, 1.0, 0.0), step.astype(jnp.float32))
    fold = masked(fold, row % MODES == lane % MODES)
    shape = (RANK * 128, 128)
    row, lane = iota(shape, 0), iota(shape, 1)
    spread = masked(jnp.where(row // 128 == lane // MODES, 1.0, 0.0), row % MODES == lane % MODES)

    shape = (256, 512)
    table_x = masked(repeat_rows(table_x_ref[...]), iota(shape, 0) % 16 == iota(shape, 1) % 16)
    scale = repeat_rows(lanes_v_ref[...])
    mixed = []
    for b in range(SLICES):
        data = got_ref[:, b * 16 : (b + 1) * 16, :].reshape(256, LANES).astype(jnp.float32)
        modes = dot(table_x, with_turned(data)) * scale
        modes = dot(modes.astype(jnp.bfloat16), fold).reshape(MODES, CHANNELS, LANES)
        real, imag = modes[..., :HALF], modes[..., HALF:]
        for h in range(2):
            lanes = slice(h * HALF, (h + 1) * HALF)
            w_real = got_ref[:, 32:48, lanes].astype(jnp.float32)
            w_imag = got_ref[:, 48:64, lanes].astype(jnp.float32)
            out_real = jnp.sum(real * w_real - imag * w_imag, axis=1)
            out_imag = jnp.sum(real * w_imag + imag * w_real, axis=1)
            mixed.append(jnp.concatenate([out_real, out_imag], axis=0))
    mixed = jnp.concatenate(mixed, axis=1)
    mixed = mixed.astype(jnp.bfloat16).astype(jnp.float32)
    back = jnp.dot(
        back_x_ref[...], mixed, precision=lax.Precision.HIGHEST, preferred_element_type=jnp.float32
    )
    own = iota((8, 128), 0) == iota((8, 128), 1) // MODES
    rows = []
    for b in range(SLICES):
        for h in range(2):
            at = (2 * b + h) * 128
            for a in range(2):
                pieces = [
                    jnp.where(own, back[a * RANK + r : a * RANK + r + 1, at : at + 128], 0.0)
                    for r in range(RANK)
                ]
                rows.append(jnp.concatenate(pieces, axis=1))
    rows = jnp.concatenate(rows, axis=0).astype(jnp.bfloat16)
    rows = dot(rows, spread).reshape(SLICES, 2, 2, 8, HALF)
    for b in range(SLICES):
        half = [jnp.concatenate([rows[b, 0, a], rows[b, 1, a]], axis=0) for a in range(2)]
        message = jnp.concatenate(half, axis=1).astype(jnp.bfloat16)
        out_ref[:, b] = jnp.broadcast_to(message[None], (Z_CHIPS, CHANNELS, LANES))


def prepare_kernel(
    skip_ref, bias_ref, own_ref, table_y_ref, basis_ref, table_z_ref,
    left_ref, parts_ref, rows_z_ref, expand_ref, other_y_ref, modes_ref,
):
    shape = (256, 256)
    place = (iota((16, 256), 0) == iota((16, 256), 1) // 16).astype(jnp.bfloat16)
    skip = repeat_rows(dot(skip_ref[...], place))
    left_ref[...] = masked(skip, iota(shape, 0) % 16 == iota(shape, 1) % 16)
    one = iota((256, 16), 0) // 16 == iota((256, 16), 1)
    bias = jnp.sum(jnp.where(one, bias_ref[...], 0.0), axis=1, keepdims=True)
    for j in range(3):
        part = bias.astype(jnp.bfloat16).astype(jnp.float32)
        parts_ref[j] = jnp.broadcast_to(part, (256, 128))
        bias = bias - part

    shape = (2 * MODES, GRID)
    ones = jnp.where(iota(shape, 0) == MODES, 1.0, 0.0)
    for j in range(GROUP):
        blocks = [ones, ones, ones, jnp.zeros(shape, jnp.float32)]
        blocks[j] = blocks[j] + table_z_ref[...]
        rows_z_ref[j] = jnp.concatenate(blocks, axis=0).astype(jnp.bfloat16)

    shape = (256, 512)
    table = masked(tile_rows(table_y_ref[...]), iota(shape, 0) // 16 == iota(shape, 1) % 16)
    expand_ref[...] = masked(repeat_rows(basis_ref[...]), iota(shape, 0) % 16 == iota(shape, 1) % 16)
    own = jnp.concatenate([table[:, 0:128], table[:, 256:384]], axis=1)
    other_y_ref[...] = jnp.concatenate([table[:, 128:256], table[:, 384:512]], axis=1)
    for b in range(SLICES):
        data = own_ref[:, b].reshape(128, LANES).astype(jnp.float32)
        modes_ref[b] = dot(own, with_turned(data))


def inverse_kernel(
    held0, held1, held2, held3, left_ref, parts_ref, table_z_ref, expand_ref, table_y_ref, modes_ref, other_ref,
    out_ref, ready, sent,
):
    held = [held0, held1, held2, held3]

    def store(g, j, count):
        return pltpu.make_async_copy(
            ready.at[g, :, :, pl.ds(j, count)],
            out_ref.at[:, :, pl.ds(g * GROUP + j, count)],
            sent.at[g + j],
        )

    skip = left_ref[...]
    tables_z = [table_z_ref[j] for j in range(GROUP)]
    lane = iota((256, 512), 1) % 128
    modes = []
    for b in range(SLICES):
        data = other_ref[:, b].reshape(128, LANES).astype(jnp.float32)
        rows = modes_ref[b] + dot(table_y_ref[...], with_turned(data))
        rows = dot(rows.astype(jnp.bfloat16), expand_ref[...])
        for j in range(3):
            part = jnp.concatenate([parts_ref[j]] * 4, axis=1)
            rows = jnp.where(lane == 32 * j + 16, part, rows)
        modes.append(rows.astype(jnp.bfloat16))

    stores = []
    for g in range(GROUPS):
        for j in range(GROUP):
            for b in range(SLICES):
                lhs = modes[b][:, g * 128 : (g + 1) * 128]
                for r in range(0, 256, ROWS):
                    value = dot(lhs[r : r + ROWS], tables_z[j])
                    value = value + dot(skip[r : r + ROWS], held[g][b, :, j].reshape(256, GRID))
                    half = 0.5 * value
                    value = half + half * lax.erf(value * math.sqrt(0.5))
                    value = value.astype(jnp.bfloat16).reshape(ROWS // BLOCK, BLOCK, GRID)
                    ready[g, b, r // BLOCK : (r + ROWS) // BLOCK, j] = value
            if g == GROUPS - 1:
                stores.append(store(g, j, 1))
            elif j == GROUP - 1:
                stores.append(store(g, 0, GROUP))
            else:
                continue
            stores[-1].start()
    for copy in stores:
        copy.wait()


VM = pl.BlockSpec(memory_space=pltpu.VMEM)
SM = pl.BlockSpec(memory_space=pltpu.SMEM)
ANY = pl.BlockSpec(memory_space=pl.ANY)
PARAMS = pltpu.CompilerParams(vmem_limit_bytes=VMEM)
PAIR = [(i, i ^ 1) for i in range(16)]
CHIPS = [[2 * chip + core for chip in CHIP_ORDER] for core in range(2)]
BLOCKS = [list(BLOCK_ORDER)]


def shape_of(shape, dtype):
    return jax.ShapeDtypeStruct(shape, dtype)


def on_device(field, spectral_weight, skip_weight, bias):
    t = make_tables()
    f32, bf16 = jnp.float32, jnp.bfloat16
    place = jnp.stack([lax.axis_index("px"), lax.axis_index("py")]).astype(jnp.int32)
    planes = (SLICES, CHANNELS, GROUP, BLOCK, GRID)
    part = (Z_CHIPS, SLICES, CHANNELS, LANES)

    far = [
        pltpu.with_memory_space_constraint(a, pltpu.HBM)
        for a in (
            field, t["forward_z"], t["lanes_x"], t["forward_y"],
            t["inverse_y"], t["inverse_x"],
        )
    ]
    sums, send, table_y, back_y, back_x, *held = pl.pallas_call(
        forward_kernel,
        name="forward",
        in_specs=[SM] + [ANY] * 6,
        out_specs=[VM] * (5 + GROUPS),
        out_shape=[
            shape_of((SLICES, 256, LANES), bf16),
            shape_of(part, bf16),
            shape_of((16, 512), f32),
            shape_of((16, 512), f32),
            shape_of((16, 32), f32),
            *[pltpu.VMEM(planes, bf16)] * GROUPS,
        ],
        scratch_shapes=[
            pltpu.VMEM((GRID, LANES), f32),
            pltpu.VMEM((BLOCK, LANES), f32),
            pltpu.VMEM((512, LANES), f32),
            pltpu.SemaphoreType.DMA((GROUPS,)),
            pltpu.SemaphoreType.DMA((5,)),
        ],
        compiler_params=PARAMS,
    )(place, *far)
    got = lax.ppermute(send, "py", PAIR)
    keep, packed = pl.pallas_call(
        keep_kernel,
        name="keep",
        in_specs=[VM, VM, VM],
        out_specs=[VM, VM],
        out_shape=[shape_of(part, f32), shape_of((32, LANES), bf16)],
        compiler_params=PARAMS,
        cost_estimate=pl.CostEstimate(flops=2 * 2 * 128 * 512 * 256, bytes_accessed=1 << 20, transcendentals=0),
    )(sums, table_y, spectral_weight.reshape(512, MODES))
    sums = (keep + got.astype(f32)).astype(bf16)
    sums = lax.all_to_all(sums, "py", 0, 0, axis_index_groups=CHIPS, tiled=True)
    message = pl.pallas_call(
        sum_kernel,
        name="sum",
        in_specs=[VM, VM],
        out_specs=VM,
        out_shape=shape_of((16, 64, LANES), bf16),
        compiler_params=PARAMS,
    )(sums, packed)
    message = lax.all_to_all(message, "px", 0, 0, axis_index_groups=BLOCKS, tiled=True)
    message = pl.pallas_call(
        mix_kernel,
        name="mix",
        in_specs=[VM, VM, VM, VM],
        out_specs=VM,
        out_shape=shape_of(part, bf16),
        compiler_params=PARAMS,
    )(message, t["forward_x"], t["lanes_v"], back_x)
    own = lax.all_to_all(message, "py", 0, 0, axis_index_groups=CHIPS, tiled=True)
    other = lax.ppermute(own, "py", PAIR)
    prepared = pl.pallas_call(
        prepare_kernel,
        name="prepare",
        in_specs=[VM] * 6,
        out_specs=[VM] * 6,
        out_shape=[
            shape_of((256, 256), bf16),
            shape_of((3, 256, 128), f32),
            shape_of((GROUP, 128, GRID), bf16),
            shape_of((LANES, 512), bf16),
            shape_of((256, 256), bf16),
            shape_of((SLICES, 256, LANES), f32),
        ],
        compiler_params=PARAMS,
        cost_estimate=pl.CostEstimate(flops=2 * 2 * 256 * 256 * 256, bytes_accessed=1 << 20, transcendentals=0),
    )(skip_weight, bias.reshape(1, 16), own, back_y, t["expand_x"], t["inverse_z"])
    return pl.pallas_call(
        inverse_kernel,
        name="inverse",
        in_specs=[VM] * (7 + GROUPS),
        out_specs=ANY,
        out_shape=shape_of(field.shape, bf16),
        scratch_shapes=[
            pltpu.VMEM((GROUPS, *planes), bf16),
            pltpu.SemaphoreType.DMA((GROUPS + GROUP - 1,)),
        ],
        compiler_params=PARAMS,
    )(*held, *prepared, other)


def solution(mesh):
    return jax.shard_map(
        on_device,
        mesh=mesh,
        in_specs=(P(None, None, "px", "py", None), P("px", "py", None, None, None, None), P(), P()),
        out_specs=P(None, None, "px", "py", None),
        check_vma=False,
    )
```
